128 devices in a mesh: blk: 32 (over z, x, core), rep: 4 (over y).
Axes of the slice: x: 4, y: 4, z: 4, core: 2. Of those that a mesh axis runs over, the one named last changes fastest.
Arguments:
- density: bfloat16 [512, 9, 128, 128], P(('blk', 'rep')), may hold values from -0.48 to 0.48, as said below
- pattern: int32 [512, 9], P(('blk', 'rep')), may hold values from 0 to 1, as said below
- orbitals: int32 [512], replicated, may hold values from 96 to 128
Outputs:
- purified: bfloat16 [512, 9, 128, 128], P(('blk', 'rep'))
The draws below stay inside these ranges and needn't reach their ends.
Inputs may be any that keep to these rules, and one draw needn't show every extreme that they name: `density`: the stored matrix is symmetric: the block at [c, s] is the transpose of the block at [(c + s - 4) mod 512, 8 - s]. The pattern is symmetric: pattern[c, s] = pattern[(c + s - 4) mod 512, 8 - s]; every diagonal block (s = 4) is 1.
All inputs are finite; a program needn't handle non-finite values.
Results may differ from the reference program's by a relative error of at most 0.0037.
Values may be sent and summed in bfloat16 or wider, within the bound.
No kernel may reach another device: no remote copies, remote signals or barrier semaphores. Data moves between devices by JAX's collectives and lax.ppermute only.
A program may use at most 64 MiB of HBM per device.

```python
import jax
import jax.numpy as jnp
from jax import lax

BLOCK = 128
REACH = 4
NBLOCKS = 512
BAND = 9


def mirrored(values):
    return jnp.stack([jnp.roll(values[:, BAND - 1 - slot], -(slot - REACH), axis=0) for slot in range(BAND)], axis=1)


def draw_density(key, part):
    key = jax.random.fold_in(key, 17)
    drawn = 0.12 * jax.random.truncated_normal(key, -4.0, 4.0, (NBLOCKS, BAND, BLOCK, BLOCK), jnp.float32)
    return (0.5 * (drawn + jnp.swapaxes(mirrored(drawn), 2, 3))).astype(jnp.bfloat16)


def draw_pattern(key, part):
    key = jax.random.fold_in(key, 29)
    drawn = jax.random.randint(key, (NBLOCKS, BAND), 0, 5)
    chosen = (drawn < 4).astype(jnp.int32)
    paired = chosen * mirrored(chosen)
    return paired.at[:, REACH].set(1)


def with_ends(values, rng, least, top_value):
    spot = [jax.random.randint(jax.random.fold_in(rng, axis), (), 0, length) for axis, length in enumerate(values.shape)]
    widest = values.shape.index(max(values.shape))
    next_to = spot[:widest] + [(spot[widest] + 1) % values.shape[widest]] + spot[widest + 1:]
    return values.at[tuple(spot)].set(least).at[tuple(next_to)].set(top_value)


def setup_inputs(seed: int = 0) -> dict:
    keys = jax.random.split(jax.random.key(seed), 4)
    return {
        "density": draw_density(jax.random.fold_in(keys[3], 71), 0),
        "pattern": draw_pattern(jax.random.fold_in(keys[3], 71), 0),
        "orbitals": with_ends(jax.random.randint(keys[2], (NBLOCKS,), BLOCK * 3 // 4, BLOCK + 1), jax.random.fold_in(keys[2], 1), BLOCK * 3 // 4, BLOCK).astype(jnp.int32),
    }


def band_rows(values):
    return jnp.stack([jnp.roll(values, -(slot - REACH)) for slot in range(BAND)], axis=1)


def masked_density(density, pattern, orbitals):
    lane_ids = jnp.arange(BLOCK, dtype=jnp.int32)
    row_counts = band_rows(orbitals)
    visible = (lane_ids[None, None, :, None] < row_counts[:, :, None, None]) & (lane_ids[None, None, None, :] < orbitals[:, None, None, None]) & (pattern[:, :, None, None] == 1)
    return jnp.where(visible, density, jnp.zeros_like(density))


def band_product(left, right):
    total = jnp.zeros(left.shape, jnp.float32)
    for step_t in range(BAND):
        first_slot = max(0, step_t - REACH)
        last_slot = min(BAND - 1, step_t + REACH)
        first_row = first_slot - step_t + REACH
        slot_count = last_slot - first_slot + 1
        moved = jnp.roll(left, -(step_t - REACH), axis=0)[:, first_row:first_row + slot_count]
        partial_sum = jnp.einsum('csab,cbd->csad', moved.astype(jnp.float32), right[:, step_t].astype(jnp.float32), precision=lax.Precision.HIGHEST)
        total = total.at[:, first_slot:last_slot + 1].add(partial_sum)
    return total


def reference(density, pattern, orbitals):
    masked = masked_density(density, pattern, orbitals)
    in_pattern = (pattern == 1)[:, :, None, None]
    square = band_product(masked, masked)
    squared = jnp.where(in_pattern, square, jnp.zeros_like(square)).astype(jnp.bfloat16)
    cube = band_product(squared, masked)
    mixed = 3.0 * square - 2.0 * cube
    return jnp.where(in_pattern, mixed, jnp.zeros_like(mixed)).astype(jnp.bfloat16)
```

```python
import jax
import jax.numpy as jnp
from jax import lax
from jax.experimental import pallas as pl
from jax.experimental.pallas import tpu as pltpu
from jax.sharding import PartitionSpec as P

AXES = ("blk", "rep")
T = 128
COLS = 4
REACH = 4
BAND = 9
SIDE = COLS * T
BELOW = [(a, b) for b in range(COLS) for a in range(b + 1, COLS)]
PACKED = (len(BELOW) + COLS // 2) * T + 16
F32 = jnp.float32
BF16 = jnp.bfloat16
LIMIT = 40 * 1024 * 1024

VMEM = pl.BlockSpec(memory_space=pltpu.VMEM)
SMEM = pl.BlockSpec(memory_space=pltpu.SMEM)
ANY = pl.BlockSpec(memory_space=pl.ANY)


def rows_cols():
    return (
        lax.broadcasted_iota(jnp.int32, (T, T), 0),
        lax.broadcasted_iota(jnp.int32, (T, T), 1),
    )


def at(index):
    return slice(index * T, (index + 1) * T)


def half(index):
    return slice(2 * index * T, 2 * (index + 1) * T)


def span(first, last):
    return slice(2 * first * T, 2 * (last + 1) * T)


def dot(a, b):
    return lax.dot_general(a, b, (((1,), (0,)), ((), ())), preferred_element_type=F32)


def dot_tn(a, b):
    return lax.dot_general(a, b, (((0,), (0,)), ((), ())), preferred_element_type=F32)


def pack(out_ref, block):
    row, col = rows_cols()
    for index, (a, b) in enumerate(BELOW):
        out_ref[at(index), :] = block(a, b).astype(BF16)
    strip_row = lax.broadcasted_iota(jnp.int32, (16, T), 0)
    strip = jnp.zeros((16, T), F32)
    for pair in range(COLS // 2):
        first = block(2 * pair, 2 * pair).astype(F32)
        second = block(2 * pair + 1, 2 * pair + 1).astype(F32)
        out_ref[at(len(BELOW) + pair), :] = jnp.where(row >= col, first, second).astype(BF16)
        diagonal = jnp.sum(jnp.where(row == col, second, 0.0), axis=0, keepdims=True)
        strip = jnp.where(strip_row == pair, diagonal, strip)
    out_ref[PACKED - 16 : PACKED, :] = strip.astype(BF16)


def unpack(packed_ref, full_ref):
    row, col = rows_cols()
    for index, (a, b) in enumerate(BELOW):
        block = packed_ref[at(index), :]
        full_ref[at(a), at(b)] = block
        full_ref[at(b), at(a)] = block.T
    strip = packed_ref[PACKED - 16 : PACKED, :].astype(F32)
    for pair in range(COLS // 2):
        both = packed_ref[at(len(BELOW) + pair), :].astype(F32)
        turned = both.T
        first = jnp.where(row >= col, both, turned)
        second = jnp.where(row < col, both, turned)
        second = jnp.where(row == col, strip[pair : pair + 1, :], second)
        full_ref[at(2 * pair), at(2 * pair)] = first.astype(BF16)
        full_ref[at(2 * pair + 1), at(2 * pair + 1)] = second.astype(BF16)


def pack_own(density, pattern, orbitals, out, held, sems):
    first = lax.axis_index(AXES) * COLS
    copies = [
        pltpu.make_async_copy(
            density.at[b, pl.ds(REACH, COLS - b)], held.at[b, pl.ds(0, COLS - b)], sems.at[b]
        )
        for b in range(COLS)
    ]
    for copy in copies:
        copy.start()
    row, col = rows_cols()
    used = [orbitals[first + a] for a in range(COLS)]
    for copy in copies:
        copy.wait()

    def block(a, b):
        visible = (row < used[a] * pattern[b, a - b + REACH]) & (col < used[b])
        return jnp.where(visible, held[b, a - b].astype(F32), 0.0)

    pack(out, block)


def own_square(density, pattern, orbitals, wide, square, squared, packed):
    count = orbitals.shape[0]
    first = lax.axis_index(AXES) * COLS
    used = [orbitals[lax.rem(first + r - REACH + count, count)] for r in range(COLS + 2 * REACH)]
    row, col = rows_cols()
    zero = jnp.zeros((T, T), BF16)
    for c in range(COLS):
        for r in range(COLS + 2 * REACH):
            if c <= r < c + BAND:
                visible = (row < used[r] * pattern[c, r - c]) & (col < used[c + REACH])
                wide[at(r), at(c)] = jnp.where(visible, density[c, r - c].astype(F32), 0.0).astype(BF16)
            else:
                wide[at(r), at(c)] = zero
    left, own, right = (wide.at[k * SIDE : (k + 1) * SIDE] for k in range(3))
    for i, j in ((0, 0), (0, 1), (1, 0), (1, 1)):
        low = max(i, j)
        high = min(i, j)
        square[half(i), half(j)] = (
            dot(own[half(i), :], own[:, half(j)])
            + dot_tn(left[span(low, 1), half(i)], left[span(low, 1), half(j)])
            + dot_tn(right[span(0, high), half(i)], right[span(0, high), half(j)])
        )
    for b in range(COLS):
        for a in range(COLS):
            squared[at(a), at(b)] = jnp.where(pattern[b, a - b + REACH] == 1, square[at(a), at(b)], 0.0).astype(BF16)
    pack(packed, lambda a, b: squared[at(a), at(b)])


def side_blocks(side, tile):
    for a in (2 * tile[0], 2 * tile[0] + 1):
        for c in (2 * tile[1], 2 * tile[1] + 1):
            if side == 0 and a >= c:
                yield a, c, a - c, a - c
            if side == 1 and a <= c:
                yield a, c, a - c + 2 * REACH, COLS - c + a


TILES = (((0, 0), (1, 0), (1, 1)), ((0, 0), (0, 1), (1, 1)))


def full_by_side(side, tile, full, thin):
    i, j = tile
    inner = span(j, 1) if side == 0 else span(0, j)
    return dot(full[half(i), inner], thin[inner, half(j)])


def side_by_full(side, tile, thin, full):
    i, j = tile
    inner = span(0, i) if side == 0 else span(i, 1)
    return dot(thin[half(i), inner], full[inner, half(j)])


def middle(packed_left, packed_right, wide, square, squared, pattern, acc, out, full, cross, tile_ref, held, sems):
    own = wide.at[SIDE : 2 * SIDE]
    for side, packed in ((0, packed_left), (1, packed_right)):
        thin = wide.at[side * 2 * SIDE : (side * 2 + 1) * SIDE]
        crossed = cross.at[side]
        unpack(packed, full)
        crossed[...] = jnp.zeros((SIDE, SIDE), BF16)
        for tile in TILES[side]:
            tile_ref[...] = full_by_side(side, tile, full, thin) + side_by_full(side, tile, thin, own)
            for a, c, slot, place in side_blocks(side, tile):
                block = tile_ref[at(a % 2), at(c % 2)]
                crossed[at(a), at(c)] = jnp.where(pattern[c, slot] == 1, block, 0.0).astype(BF16)
                acc[c, place] = 3.0 * block
        for tile in TILES[side]:
            tile_ref[...] = side_by_full(side, tile, crossed, own)
            for a, c, slot, place in side_blocks(side, tile):
                acc[c, place] = acc[c, place] - 2.0 * tile_ref[at(a % 2), at(c % 2)]
    left, right = wide.at[:SIDE], wide.at[2 * SIDE :]
    for j in range(2):
        for i in range(2):
            low, high = span(max(i, j), 1), span(0, min(i, j))
            tile_ref[...] = (
                dot(squared[half(i), :], own[:, half(j)])
                + dot_tn(cross[0, low, half(i)], left[low, half(j)])
                + dot_tn(cross[1, high, half(i)], right[high, half(j)])
            )
            for a in (2 * i, 2 * i + 1):
                for c in (2 * j, 2 * j + 1):
                    mixed = 3.0 * square[at(a), at(c)] - 2.0 * tile_ref[at(a % 2), at(c % 2)]
                    held[c, a] = jnp.where(pattern[c, a - c + REACH] == 1, mixed, 0.0).astype(BF16)
    copies = [
        pltpu.make_async_copy(held.at[c], out.at[c, pl.ds(REACH - c, COLS)], sems.at[c]) for c in range(COLS)
    ]
    for copy in copies:
        copy.start()
    for copy in copies:
        copy.wait()


def finish(packed_left, packed_right, wide, acc, pattern, begun, out, full, tile_ref, held, sems):
    del begun
    copies = []
    for side, packed in ((0, packed_left), (1, packed_right)):
        thin = wide.at[side * 2 * SIDE : (side * 2 + 1) * SIDE]
        unpack(packed, full)
        for tile in TILES[side]:
            tile_ref[...] = full_by_side(side, tile, full, thin)
            for a, c, slot, place in side_blocks(side, tile):
                mixed = acc[c, place] - 2.0 * tile_ref[at(a % 2), at(c % 2)]
                held[c, place] = jnp.where(pattern[c, slot] == 1, mixed, 0.0).astype(BF16)
        for c in range(COLS):
            place, slot, many = (0, 0, COLS - c) if side == 0 else (COLS - c, 2 * REACH - c, c + 1)
            copy = pltpu.make_async_copy(
                held.at[c, pl.ds(place, many)], out.at[c, pl.ds(slot, many)], sems.at[side, c]
            )
            copy.start()
            copies.append(copy)
    for copy in copies:
        copy.wait()


def call(kernel, outs, ins, out_specs, scratch, flops, moved, **more):
    return pl.pallas_call(
        kernel,
        out_shape=outs,
        in_specs=ins,
        out_specs=out_specs,
        scratch_shapes=scratch,
        compiler_params=pltpu.CompilerParams(vmem_limit_bytes=LIMIT),
        cost_estimate=pl.CostEstimate(flops=flops, bytes_accessed=moved, transcendentals=0),
        **more,
    )


def shape(*dims, dtype=BF16):
    return jax.ShapeDtypeStruct(dims, dtype)


def per_device(density, pattern, orbitals):
    count = lax.axis_size(AXES)

    def to_right(array):
        return lax.ppermute(array, AXES, [(i, (i + 1) % count) for i in range(count)])

    def to_left(array):
        return lax.ppermute(array, AXES, [(i, (i - 1) % count) for i in range(count)])

    packed = call(
        pack_own,
        shape(PACKED, T),
        [ANY, SMEM, SMEM],
        VMEM,
        [pltpu.VMEM((COLS, COLS, T, T), BF16), pltpu.SemaphoreType.DMA((COLS,))],
        0,
        2**20,
    )(density, pattern, orbitals)
    own_left, own_right = to_right(packed), to_left(packed)
    wide, square, squared, packed_square = call(
        own_square,
        (shape(3 * SIDE, SIDE), shape(SIDE, SIDE, dtype=F32), shape(SIDE, SIDE), shape(PACKED, T)),
        [VMEM, SMEM, SMEM],
        (VMEM,) * 4,
        [],
        2**30,
        2**22,
    )(density, pattern, orbitals)
    square_left, square_right = to_right(packed_square), to_left(packed_square)
    acc, begun = call(
        middle,
        (shape(COLS, COLS + 1, T, T, dtype=F32), shape(*density.shape)),
        [VMEM, VMEM, VMEM, VMEM, VMEM, SMEM],
        (VMEM, ANY),
        [
            pltpu.VMEM((SIDE, SIDE), BF16),
            pltpu.VMEM((2, SIDE, SIDE), BF16),
            pltpu.VMEM((2 * T, 2 * T), F32),
            pltpu.VMEM((COLS, COLS, T, T), BF16),
            pltpu.SemaphoreType.DMA((COLS,)),
        ],
        2**31,
        2**22,
    )(own_left, own_right, wide, square, squared, pattern)
    return call(
        finish,
        shape(*density.shape),
        [VMEM, VMEM, VMEM, VMEM, SMEM, ANY],
        ANY,
        [
            pltpu.VMEM((SIDE, SIDE), BF16),
            pltpu.VMEM((2 * T, 2 * T), F32),
            pltpu.VMEM((COLS, COLS + 1, T, T), BF16),
            pltpu.SemaphoreType.DMA((2, COLS)),
        ],
        2**29,
        2**22,
        input_output_aliases={5: 0},
    )(square_left, square_right, wide, acc, pattern, begun)


def solution(mesh):
    placed = (P(AXES, None, None, None), P(AXES, None), P())
    return jax.shard_map(
        per_device, mesh=mesh, in_specs=placed, out_specs=P(AXES, None, None, None), check_vma=False
    )
```

```python
import functools

import jax
import jax.numpy as jnp
from jax import lax
from jax.experimental import pallas as pl
from jax.experimental.pallas import tpu as pltpu
from jax.sharding import PartitionSpec as P

AXES = ("blk", "rep")
T = 128
COLS = 4
REACH = 4
BAND = 9
SIDE = COLS * T
BELOW = [(a, b) for b in range(COLS) for a in range(b + 1, COLS)]
PACKED = (len(BELOW) + COLS // 2) * T + 16
F32 = jnp.float32
BF16 = jnp.bfloat16
LIMIT = 40 * 1024 * 1024

VMEM = pl.BlockSpec(memory_space=pltpu.VMEM)
SMEM = pl.BlockSpec(memory_space=pltpu.SMEM)
ANY = pl.BlockSpec(memory_space=pl.ANY)


def rows_cols():
    return (
        lax.broadcasted_iota(jnp.int32, (T, T), 0),
        lax.broadcasted_iota(jnp.int32, (T, T), 1),
    )


def at(index):
    return slice(index * T, (index + 1) * T)


def half(index):
    return slice(2 * index * T, 2 * (index + 1) * T)


def span(first, last):
    return slice(2 * first * T, 2 * (last + 1) * T)


def dot(a, b):
    return lax.dot_general(a, b, (((1,), (0,)), ((), ())), preferred_element_type=F32)


def dot_tn(a, b):
    return lax.dot_general(a, b, (((0,), (0,)), ((), ())), preferred_element_type=F32)


def pack(out_ref, block):
    row, col = rows_cols()
    for index, (a, b) in enumerate(BELOW):
        out_ref[at(index), :] = block(a, b).astype(BF16)
    strip_row = lax.broadcasted_iota(jnp.int32, (16, T), 0)
    strip = jnp.zeros((16, T), F32)
    for pair in range(COLS // 2):
        first = block(2 * pair, 2 * pair).astype(F32)
        second = block(2 * pair + 1, 2 * pair + 1).astype(F32)
        out_ref[at(len(BELOW) + pair), :] = jnp.where(row >= col, first, second).astype(BF16)
        diagonal = jnp.sum(jnp.where(row == col, second, 0.0), axis=0, keepdims=True)
        strip = jnp.where(strip_row == pair, diagonal, strip)
    out_ref[PACKED - 16 : PACKED, :] = strip.astype(BF16)


def unpack(packed_ref, full_ref):
    row, col = rows_cols()
    for index, (a, b) in enumerate(BELOW):
        block = packed_ref[at(index), :]
        full_ref[at(a), at(b)] = block
        full_ref[at(b), at(a)] = block.T
    strip = packed_ref[PACKED - 16 : PACKED, :].astype(F32)
    for pair in range(COLS // 2):
        both = packed_ref[at(len(BELOW) + pair), :].astype(F32)
        turned = both.T
        first = jnp.where(row >= col, both, turned)
        second = jnp.where(row < col, both, turned)
        second = jnp.where(row == col, strip[pair : pair + 1, :], second)
        full_ref[at(2 * pair), at(2 * pair)] = first.astype(BF16)
        full_ref[at(2 * pair + 1), at(2 * pair + 1)] = second.astype(BF16)


def load(pairs, sems):
    copies = [pltpu.make_async_copy(source, target, sems.at[i]) for i, (source, target) in enumerate(pairs)]
    for copy in copies:
        copy.start()
    return copies


def pack_own(density, pattern, orbitals, out, held, pattern_now, orbitals_now, sems):
    first = lax.axis_index(AXES) * COLS
    pairs = [(density.at[b, pl.ds(REACH, COLS - b)], held.at[b, pl.ds(0, COLS - b)]) for b in range(COLS)]
    copies = load([(orbitals, orbitals_now), (pattern, pattern_now)] + pairs, sems)
    row, col = rows_cols()
    for copy in copies:
        copy.wait()
    used = [orbitals_now[first + a] for a in range(COLS)]

    def block(a, b):
        visible = (row < used[a] * pattern_now[b, a - b + REACH]) & (col < used[b])
        return jnp.where(visible, held[b, a - b].astype(F32), 0.0)

    pack(out, block)


def own_square(density, pattern_far, orbitals_far, wide, square, squared, packed, kept, pattern, orbitals, sems):
    for copy in load([(orbitals_far, orbitals), (pattern_far, pattern)], sems):
        copy.wait()
    for c in range(COLS):
        for slot in range(BAND):
            kept[c * BAND + slot : c * BAND + slot + 1, :] = jnp.full((1, T), pattern[c, slot], jnp.int32)
    count = orbitals.shape[0]
    first = lax.axis_index(AXES) * COLS
    used = [orbitals[lax.rem(first + r - REACH + count, count)] for r in range(COLS + 2 * REACH)]
    row, col = rows_cols()
    zero = jnp.zeros((T, T), BF16)
    for c in range(COLS):
        for r in range(COLS + 2 * REACH):
            if c <= r < c + BAND:
                visible = (row < used[r] * pattern[c, r - c]) & (col < used[c + REACH])
                wide[at(r), at(c)] = jnp.where(visible, density[c, r - c].astype(F32), 0.0).astype(BF16)
            else:
                wide[at(r), at(c)] = zero
    left, own, right = (wide.at[k * SIDE : (k + 1) * SIDE] for k in range(3))
    for i, j in ((0, 0), (0, 1), (1, 0), (1, 1)):
        low = max(i, j)
        high = min(i, j)
        square[half(i), half(j)] = (
            dot(own[half(i), :], own[:, half(j)])
            + dot_tn(left[span(low, 1), half(i)], left[span(low, 1), half(j)])
            + dot_tn(right[span(0, high), half(i)], right[span(0, high), half(j)])
        )
    for b in range(COLS):
        for a in range(COLS):
            squared[at(a), at(b)] = jnp.where(pattern[b, a - b + REACH] == 1, square[at(a), at(b)], 0.0).astype(BF16)
    pack(packed, lambda a, b: squared[at(a), at(b)])


def side_blocks(side, tile):
    for a in (2 * tile[0], 2 * tile[0] + 1):
        for c in (2 * tile[1], 2 * tile[1] + 1):
            if side == 0 and a >= c:
                yield a, c, a - c, a - c
            if side == 1 and a <= c:
                yield a, c, a - c + 2 * REACH, COLS - c + a


def keep(kept, c, slot):
    return kept[c * BAND + slot : c * BAND + slot + 1, :] == 1


TILES = (((0, 0), (1, 0), (1, 1)), ((0, 0), (0, 1), (1, 1)))


def full_by_side(side, tile, full, thin):
    i, j = tile
    inner = span(j, 1) if side == 0 else span(0, j)
    return dot(full[half(i), inner], thin[inner, half(j)])


def side_by_full(side, tile, thin, full):
    i, j = tile
    inner = span(0, i) if side == 0 else span(i, 1)
    return dot(thin[half(i), inner], full[inner, half(j)])


def middle(packed_first, packed_second, wide, square, squared, kept, acc, out, both, cross, tile_ref, held, sems):
    own = wide.at[SIDE : 2 * SIDE]
    odd = lax.rem(lax.axis_index(AXES), 2)
    unpack(packed_first, both.at[1 - odd])
    unpack(packed_second, both.at[odd])
    for side in range(2):
        full = both.at[side]
        thin = wide.at[side * 2 * SIDE : (side * 2 + 1) * SIDE]
        crossed = cross.at[side]
        crossed[...] = jnp.zeros((SIDE, SIDE), BF16)
        for tile in TILES[side]:
            tile_ref[...] = full_by_side(side, tile, full, thin) + side_by_full(side, tile, thin, own)
            for a, c, slot, place in side_blocks(side, tile):
                block = tile_ref[at(a % 2), at(c % 2)]
                crossed[at(a), at(c)] = jnp.where(keep(kept, c, slot), block, 0.0).astype(BF16)
                acc[c, place] = 3.0 * block
        for tile in TILES[side]:
            tile_ref[...] = side_by_full(side, tile, crossed, own)
            for a, c, slot, place in side_blocks(side, tile):
                acc[c, place] = acc[c, place] - 2.0 * tile_ref[at(a % 2), at(c % 2)]
    left, right = wide.at[:SIDE], wide.at[2 * SIDE :]
    for j in range(2):
        for i in range(2):
            low, high = span(max(i, j), 1), span(0, min(i, j))
            tile_ref[...] = (
                dot(squared[half(i), :], own[:, half(j)])
                + dot_tn(cross[0, low, half(i)], left[low, half(j)])
                + dot_tn(cross[1, high, half(i)], right[high, half(j)])
            )
            for a in (2 * i, 2 * i + 1):
                for c in (2 * j, 2 * j + 1):
                    mixed = 3.0 * square[at(a), at(c)] - 2.0 * tile_ref[at(a % 2), at(c % 2)]
                    held[c, a] = jnp.where(keep(kept, c, a - c + REACH), mixed, 0.0).astype(BF16)
    copies = [
        pltpu.make_async_copy(held.at[c], out.at[c, pl.ds(REACH - c, COLS)], sems.at[c]) for c in range(COLS)
    ]
    for copy in copies:
        copy.start()
    for copy in copies:
        copy.wait()


def finish(turn, packed, wide, acc, kept, begun, out, full, tile_ref, held, sems):
    del begun
    odd = lax.rem(lax.axis_index(AXES), 2)
    unpack(packed, full)

    def one(side):
        thin = wide.at[side * 2 * SIDE : (side * 2 + 1) * SIDE]
        for tile in TILES[side]:
            tile_ref[...] = full_by_side(side, tile, full, thin)
            for a, c, slot, place in side_blocks(side, tile):
                mixed = acc[c, place] - 2.0 * tile_ref[at(a % 2), at(c % 2)]
                held[c, place] = jnp.where(keep(kept, c, slot), mixed, 0.0).astype(BF16)
        copies = []
        for c in range(COLS):
            place, slot, many = (0, 0, COLS - c) if side == 0 else (COLS - c, 2 * REACH - c, c + 1)
            copies.append(
                pltpu.make_async_copy(held.at[c, pl.ds(place, many)], out.at[c, pl.ds(slot, many)], sems.at[c])
            )
            copies[-1].start()
        for copy in copies:
            copy.wait()

    @pl.when(odd == turn)
    def _():
        one(1)

    @pl.when(odd != turn)
    def _():
        one(0)


def call(kernel, outs, ins, out_specs, scratch, flops, moved, **more):
    return pl.pallas_call(
        kernel,
        out_shape=outs,
        in_specs=ins,
        out_specs=out_specs,
        scratch_shapes=scratch,
        compiler_params=pltpu.CompilerParams(vmem_limit_bytes=LIMIT),
        cost_estimate=pl.CostEstimate(flops=flops, bytes_accessed=moved, transcendentals=0),
        **more,
    )


def shape(*dims, dtype=BF16):
    return jax.ShapeDtypeStruct(dims, dtype)


def per_device(density, pattern, orbitals):
    count = lax.axis_size(AXES)

    def exchange(array):
        first = [(i, i ^ 1) for i in range(count)]
        second = [(i, (i + 1 if i % 2 else i - 1) % count) for i in range(count)]
        return lax.ppermute(array, AXES, first), lax.ppermute(array, AXES, second)

    far = [pltpu.with_memory_space_constraint(array, pltpu.HBM) for array in (density, pattern, orbitals)]
    small = [pltpu.SMEM(pattern.shape, jnp.int32), pltpu.SMEM(orbitals.shape, jnp.int32)]
    packed = call(
        pack_own,
        shape(PACKED, T),
        [ANY] * 3,
        VMEM,
        [pltpu.VMEM((COLS, COLS, T, T), BF16), *small, pltpu.SemaphoreType.DMA((COLS + 2,))],
        0,
        2**20,
    )(*far)
    own_first, own_second = exchange(packed)
    wide, square, squared, packed_square, kept = call(
        own_square,
        (
            shape(3 * SIDE, SIDE),
            shape(SIDE, SIDE, dtype=F32),
            shape(SIDE, SIDE),
            shape(PACKED, T),
            shape(40, T, dtype=jnp.int32),
        ),
        [VMEM, ANY, ANY],
        (VMEM,) * 5,
        [*small, pltpu.SemaphoreType.DMA((2,))],
        2**30,
        2**22,
    )(density, *far[1:])
    square_first, square_second = exchange(packed_square)
    acc, begun = call(
        middle,
        (shape(COLS, COLS + 1, T, T, dtype=F32), shape(*density.shape)),
        [VMEM] * 6,
        (VMEM, ANY),
        [
            pltpu.VMEM((2, SIDE, SIDE), BF16),
            pltpu.VMEM((2, SIDE, SIDE), BF16),
            pltpu.VMEM((2 * T, 2 * T), F32),
            pltpu.VMEM((COLS, COLS, T, T), BF16),
            pltpu.SemaphoreType.DMA((COLS,)),
        ],
        2**31,
        2**22,
    )(own_first, own_second, wide, square, squared, kept)
    out = begun
    for turn, packed in enumerate((square_first, square_second)):
        out = call(
            functools.partial(finish, turn),
            shape(*density.shape),
            [VMEM] * 4 + [ANY],
            ANY,
            [
                pltpu.VMEM((SIDE, SIDE), BF16),
                pltpu.VMEM((2 * T, 2 * T), F32),
                pltpu.VMEM((COLS, COLS + 1, T, T), BF16),
                pltpu.SemaphoreType.DMA((COLS,)),
            ],
            2**28,
            2**21,
            input_output_aliases={4: 0},
        )(packed, wide, acc, kept, out)
    return out


def solution(mesh):
    placed = (P(AXES, None, None, None), P(AXES, None), P())
    return jax.shard_map(
        per_device, mesh=mesh, in_specs=placed, out_specs=P(AXES, None, None, None), check_vma=False
    )
```

```python
import jax
import jax.numpy as jnp
from jax import lax
from jax.experimental import pallas as pl
from jax.experimental.pallas import tpu as pltpu
from jax.sharding import PartitionSpec as P

AXES = ("blk", "rep")
T = 128
COLS = 4
REACH = 4
BAND = 9
SIDE = COLS * T
BELOW = [(a, b) for b in range(COLS) for a in range(b + 1, COLS)]
PACKED = (len(BELOW) + COLS // 2) * T + 16
F32 = jnp.float32
BF16 = jnp.bfloat16
LIMIT = 40 * 1024 * 1024

VMEM = pl.BlockSpec(memory_space=pltpu.VMEM)
SMEM = pl.BlockSpec(memory_space=pltpu.SMEM)
ANY = pl.BlockSpec(memory_space=pl.ANY)


def rows_cols():
    return (
        lax.broadcasted_iota(jnp.int32, (T, T), 0),
        lax.broadcasted_iota(jnp.int32, (T, T), 1),
    )


def at(index):
    return slice(index * T, (index + 1) * T)


def dot(a, b):
    return lax.dot_general(a, b, (((1,), (0,)), ((), ())), preferred_element_type=F32)


def dot_tn(a, b):
    return lax.dot_general(a, b, (((0,), (0,)), ((), ())), preferred_element_type=F32)


def pack(out_ref, block):
    row, col = rows_cols()
    for index, (a, b) in enumerate(BELOW):
        out_ref[at(index), :] = block(a, b).astype(BF16)
    strip_row = lax.broadcasted_iota(jnp.int32, (16, T), 0)
    strip = jnp.zeros((16, T), F32)
    for pair in range(COLS // 2):
        first = block(2 * pair, 2 * pair).astype(F32)
        second = block(2 * pair + 1, 2 * pair + 1).astype(F32)
        out_ref[at(len(BELOW) + pair), :] = jnp.where(row >= col, first, second).astype(BF16)
        diagonal = jnp.sum(jnp.where(row == col, second, 0.0), axis=0, keepdims=True)
        strip = jnp.where(strip_row == pair, diagonal, strip)
    out_ref[PACKED - 16 : PACKED, :] = strip.astype(BF16)


def unpack(read, full_ref):
    row, col = rows_cols()
    for index, (a, b) in enumerate(BELOW):
        block = read(at(index))
        full_ref[at(a), at(b)] = block
        full_ref[at(b), at(a)] = block.T
    strip = read(slice(PACKED - 16, PACKED)).astype(F32)
    for pair in range(COLS // 2):
        both = read(at(len(BELOW) + pair)).astype(F32)
        turned = both.T
        first = jnp.where(row >= col, both, turned)
        second = jnp.where(row < col, both, turned)
        second = jnp.where(row == col, strip[pair : pair + 1, :], second)
        full_ref[at(2 * pair), at(2 * pair)] = first.astype(BF16)
        full_ref[at(2 * pair + 1), at(2 * pair + 1)] = second.astype(BF16)


def load(pairs, sems):
    copies = [pltpu.make_async_copy(source, target, sems.at[i]) for i, (source, target) in enumerate(pairs)]
    for copy in copies:
        copy.start()
    return copies


def pack_own(density, pattern, orbitals, out, held, pattern_now, orbitals_now, sems):
    first = lax.axis_index(AXES) * COLS
    pairs = [(density.at[b, pl.ds(REACH, COLS - b)], held.at[b, pl.ds(0, COLS - b)]) for b in range(COLS)]
    copies = load([(orbitals, orbitals_now), (pattern, pattern_now)] + pairs, sems)
    row, col = rows_cols()
    for copy in copies:
        copy.wait()
    used = [orbitals_now[first + a] for a in range(COLS)]

    def block(a, b):
        visible = (row < used[a] * pattern_now[b, a - b + REACH]) & (col < used[b])
        return jnp.where(visible, held[b, a - b].astype(F32), 0.0)

    pack(out, block)


def span(first, last):
    return slice(2 * first * T, 2 * (last + 1) * T)


RANGE = ((span(0, 1), span(1, 1)), (span(0, 0), span(0, 1)))
HALVES = (span(0, 0), span(1, 1))


def side_blocks(side):
    place = 0
    for c in range(COLS):
        for a in range(c, COLS) if side == 0 else range(c + 1):
            yield a, c, a - c + 2 * REACH * side, place
            place += 1


def keep(kept, c, slot):
    return kept[c * BAND + slot : c * BAND + slot + 1, :] == 1


def side_of(wide, side):
    return wide.at[side * 2 * SIDE : (side * 2 + 1) * SIDE]


def side_by_own(side, thin, own, out):
    if side == 0:
        out[HALVES[0], HALVES[0]] = dot(thin[HALVES[0], HALVES[0]], own[HALVES[0], HALVES[0]])
        out[HALVES[1], :] = dot(thin[HALVES[1], :], own[...])
    else:
        out[HALVES[0], :] = dot(thin[HALVES[0], :], own[...])
        out[HALVES[1], HALVES[1]] = dot(thin[HALVES[1], HALVES[1]], own[HALVES[1], HALVES[1]])


def full_by_side(side, half_col, full, thin):
    rows = RANGE[side][half_col]
    return dot(full[rows, rows], thin[rows, HALVES[half_col]])


def add_turned(side, left, right, out):
    if side == 0:
        out[HALVES[0], HALVES[0]] += dot_tn(left[:, HALVES[0]], right[:, HALVES[0]])
        out[HALVES[0], HALVES[1]] += dot_tn(left[HALVES[1], HALVES[0]], right[HALVES[1], HALVES[1]])
        out[HALVES[1], :] += dot_tn(left[HALVES[1], HALVES[1]], right[HALVES[1], :])
    else:
        out[HALVES[0], :] += dot_tn(left[HALVES[0], HALVES[0]], right[HALVES[0], :])
        out[HALVES[1], HALVES[0]] += dot_tn(left[HALVES[0], HALVES[1]], right[HALVES[0], HALVES[0]])
        out[HALVES[1], HALVES[1]] += dot_tn(left[:, HALVES[1]], right[:, HALVES[1]])


def own_square(
    density, pattern_far, orbitals_far, packed_own, wide, square, packed, packed_both, kept, local, cube, pattern, orbitals, squared, sems
):
    copies = load([(orbitals_far, orbitals), (pattern_far, pattern)], sems)
    packed_both[:PACKED, :] = packed_own[...]
    for copy in copies:
        copy.wait()
    for c in range(COLS):
        for slot in range(BAND):
            kept[c * BAND + slot : c * BAND + slot + 1, :] = jnp.full((1, T), pattern[c, slot], jnp.int32)
    count = orbitals.shape[0]
    first = lax.axis_index(AXES) * COLS
    used = [orbitals[lax.rem(first + r - REACH + count, count)] for r in range(COLS + 2 * REACH)]
    row, col = rows_cols()
    zero = jnp.zeros((T, T), BF16)
    for c in range(COLS):
        for r in range(COLS + 2 * REACH):
            if c <= r < c + BAND:
                visible = (row < used[r] * pattern[c, r - c]) & (col < used[c + REACH])
                wide[at(r), at(c)] = jnp.where(visible, density[c, r - c].astype(F32), 0.0).astype(BF16)
            else:
                wide[at(r), at(c)] = zero
    own = wide.at[SIDE : 2 * SIDE]
    square[...] = dot(own[...], own[...])
    for side in range(2):
        add_turned(side, side_of(wide, side), side_of(wide, side), square)
    for b in range(COLS):
        for a in range(COLS):
            squared[at(a), at(b)] = jnp.where(pattern[b, a - b + REACH] == 1, square[at(a), at(b)], 0.0).astype(BF16)
    pack(packed, lambda a, b: squared[at(a), at(b)])
    packed_both[PACKED:, :] = packed[...]
    cube[...] = dot(squared[...], own[...])
    for side in range(2):
        side_by_own(side, side_of(wide, side), own, local.at[side])


def by_side(turn, one):
    odd = lax.rem(lax.axis_index(AXES), 2)

    @pl.when(odd == turn)
    def _():
        one(1)

    @pl.when(odd != turn)
    def _():
        one(0)


def second_reader(swapped, to_first, to_last, offset):
    me = lax.axis_index(AXES)
    last = lax.axis_size(AXES) - 1

    def read(rows):
        late = to_last[rows.start + offset : rows.stop + offset, :]
        return jnp.where(me == 0, to_first[rows, :], jnp.where(me == last, late, swapped[rows, :]))

    return read


def cross_step(side, full, wide, kept, local, crossed, acc, cube):
    thin, own = side_of(wide, side), wide.at[SIDE : 2 * SIDE]
    for j in range(2):
        local[side, RANGE[side][j], HALVES[j]] += full_by_side(side, j, full, thin)
    crossed[...] = jnp.zeros((SIDE, SIDE), BF16)
    for a, c, slot, place in side_blocks(side):
        crossed[at(a), at(c)] = jnp.where(keep(kept, c, slot), local[side, at(a), at(c)], 0.0).astype(BF16)
    side_by_own(side, crossed, own, acc)
    for a, c, slot, place in side_blocks(side):
        acc[at(a), at(c)] = 3.0 * local[side, at(a), at(c)] - 2.0 * acc[at(a), at(c)]
    add_turned(side, crossed, thin, cube)


def cross_first(packed, wide, kept, local_far, cube_far, acc, cube, full, local, crossed):
    unpack(lambda rows: packed[rows, :], full)
    cube[...] = cube_far[...]

    def one(side):
        local[side] = local_far[side]
        cross_step(side, full, wide, kept, local, crossed, acc, cube)

    by_side(0, one)


def cross_second(
    packed, to_first, to_last, wide, kept, local_far, cube_far, square, acc, out, cube, full, local, crossed, held, sems
):
    unpack(second_reader(packed, to_first, to_last, 0), full)
    cube[...] = cube_far[...]

    def one(side):
        local[side] = local_far[side]
        cross_step(side, full, wide, kept, local, crossed, acc, cube)

    by_side(1, one)
    copies = []
    for c in range(COLS):
        for a in range(COLS):
            mixed = 3.0 * square[at(a), at(c)] - 2.0 * cube[at(a), at(c)]
            held[c, a] = jnp.where(keep(kept, c, a - c + REACH), mixed, 0.0).astype(BF16)
        copies.append(pltpu.make_async_copy(held.at[c], out.at[c, pl.ds(REACH - c, COLS)], sems.at[c]))
        copies[-1].start()
    for copy in copies:
        copy.wait()


def finish(
    packed_first, packed_second, to_first, to_last, wide, kept, acc_first, acc_second, begun, out, full, held, sems
):
    del begun
    unpack(lambda rows: packed_first[rows, :], full.at[0])
    unpack(second_reader(packed_second, to_first, to_last, PACKED), full.at[1])

    def one(turn, acc, side):
        thin = side_of(wide, side)
        cross = [full_by_side(side, j, full.at[turn], thin) for j in range(2)]
        copies = []
        start = 0
        blocks = list(side_blocks(side))
        for c in range(COLS):
            here = [block for block in blocks if block[1] == c]
            for a, _, slot, place in here:
                top = a * T - RANGE[side][c // 2].start
                mixed = acc[at(a), at(c)] - 2.0 * cross[c // 2][top : top + T, at(c % 2)]
                held[turn, place] = jnp.where(keep(kept, c, slot), mixed, 0.0).astype(BF16)
            copies.append(
                pltpu.make_async_copy(
                    held.at[turn, pl.ds(here[0][3], len(here))],
                    out.at[c, pl.ds(here[0][2], len(here))],
                    sems.at[turn, c],
                )
            )
            copies[-1].start()
        return copies

    def both(side):
        for copy in one(0, acc_first, side) + one(1, acc_second, 1 - side):
            copy.wait()

    by_side(0, both)


def call(kernel, outs, ins, out_specs, scratch, flops, moved, **more):
    return pl.pallas_call(
        kernel,
        out_shape=outs,
        in_specs=ins,
        out_specs=out_specs,
        scratch_shapes=scratch,
        compiler_params=pltpu.CompilerParams(vmem_limit_bytes=LIMIT),
        cost_estimate=pl.CostEstimate(flops=flops, bytes_accessed=moved, transcendentals=0),
        **more,
    )


def shape(*dims, dtype=BF16):
    return jax.ShapeDtypeStruct(dims, dtype)


def per_device(density, pattern, orbitals):
    count = lax.axis_size(AXES)
    pairs = [(i, i ^ 1) for i in range(count)]
    others = [(i, i + 1 if i % 2 else i - 1) for i in range(1, count - 1)]
    last = count - 1

    def send(array, to):
        return lax.ppermute(array, AXES, to)

    far = [pltpu.with_memory_space_constraint(array, pltpu.HBM) for array in (density, pattern, orbitals)]
    small = [pltpu.SMEM(pattern.shape, jnp.int32), pltpu.SMEM(orbitals.shape, jnp.int32)]
    whole = pltpu.VMEM((SIDE, SIDE), BF16)
    wide_f32 = shape(SIDE, SIDE, dtype=F32)
    packed = call(
        pack_own,
        shape(PACKED, T),
        [ANY] * 3,
        VMEM,
        [pltpu.VMEM((COLS, COLS, T, T), BF16), *small, pltpu.SemaphoreType.DMA((COLS + 2,))],
        0,
        2**20,
    )(*far)
    own_first = send(packed, pairs)
    own_to_first = send(packed, [(last, 0)])
    own_second = send(packed, others)
    wide, square, packed_square, packed_both, kept, local, cube = call(
        own_square,
        (
            shape(3 * SIDE, SIDE),
            wide_f32,
            shape(PACKED, T),
            shape(2 * PACKED, T),
            shape(40, T, dtype=jnp.int32),
            shape(2, SIDE, SIDE, dtype=F32),
            wide_f32,
        ),
        [VMEM, ANY, ANY, VMEM],
        (VMEM,) * 7,
        [*small, whole, pltpu.SemaphoreType.DMA((2,))],
        2**30,
        2**22,
    )(density, *far[1:], packed)
    square_first = send(packed_square, pairs)
    square_to_first = send(packed_square, [(last, 0)])
    square_second = send(packed_square, others)
    to_last = send(packed_both, [(0, last)])
    crossing = [whole, pltpu.VMEM((2, SIDE, SIDE), F32), whole]
    acc_first, cube = call(
        cross_first,
        (wide_f32, wide_f32),
        [VMEM] * 5,
        (VMEM, VMEM),
        crossing,
        2**30,
        2**21,
    )(own_first, wide, kept, local, cube)
    acc_second, begun = call(
        cross_second,
        (wide_f32, shape(*density.shape)),
        [VMEM] * 8,
        (VMEM, ANY),
        [
            pltpu.VMEM((SIDE, SIDE), F32),
            *crossing,
            pltpu.VMEM((COLS, COLS, T, T), BF16),
            pltpu.SemaphoreType.DMA((COLS,)),
        ],
        2**30,
        2**21,
    )(own_second, own_to_first, to_last, wide, kept, local, cube, square)
    return call(
        finish,
        shape(*density.shape),
        [VMEM] * 8 + [ANY],
        ANY,
        [
            pltpu.VMEM((2, SIDE, SIDE), BF16),
            pltpu.VMEM((2, 10, T, T), BF16),
            pltpu.SemaphoreType.DMA((2, COLS)),
        ],
        2**28,
        2**21,
        input_output_aliases={8: 0},
    )(square_first, square_second, square_to_first, to_last, wide, kept, acc_first, acc_second, begun)


def solution(mesh):
    placed = (P(AXES, None, None, None), P(AXES, None), P())
    return jax.shard_map(
        per_device, mesh=mesh, in_specs=placed, out_specs=P(AXES, None, None, None), check_vma=False
    )
```

```python
import jax
import jax.numpy as jnp
from jax import lax
from jax.experimental import pallas as pl
from jax.experimental.pallas import tpu as pltpu
from jax.sharding import PartitionSpec as P

AXES = ("blk", "rep")
T = 128
COLS = 4
REACH = 4
BAND = 9
SIDE = COLS * T
BELOW = [(a, b) for b in range(COLS) for a in range(b + 1, COLS)]
PACKED = (len(BELOW) + COLS // 2) * T + 16
F32 = jnp.float32
BF16 = jnp.bfloat16
LIMIT = 40 * 1024 * 1024

VMEM = pl.BlockSpec(memory_space=pltpu.VMEM)
SMEM = pl.BlockSpec(memory_space=pltpu.SMEM)
ANY = pl.BlockSpec(memory_space=pl.ANY)


def rows_cols():
    return (
        lax.broadcasted_iota(jnp.int32, (T, T), 0),
        lax.broadcasted_iota(jnp.int32, (T, T), 1),
    )


def at(index):
    return slice(index * T, (index + 1) * T)


def dot(a, b):
    return lax.dot_general(a, b, (((1,), (0,)), ((), ())), preferred_element_type=F32)


def dot_tn(a, b):
    return lax.dot_general(a, b, (((0,), (0,)), ((), ())), preferred_element_type=F32)


def pack(out_ref, block):
    row, col = rows_cols()
    for index, (a, b) in enumerate(BELOW):
        out_ref[at(index), :] = block(a, b).astype(BF16)
    strip_row = lax.broadcasted_iota(jnp.int32, (16, T), 0)
    strip = jnp.zeros((16, T), F32)
    for pair in range(COLS // 2):
        first = block(2 * pair, 2 * pair).astype(F32)
        second = block(2 * pair + 1, 2 * pair + 1).astype(F32)
        out_ref[at(len(BELOW) + pair), :] = jnp.where(row >= col, first, second).astype(BF16)
        diagonal = jnp.sum(jnp.where(row == col, second, 0.0), axis=0, keepdims=True)
        strip = jnp.where(strip_row == pair, diagonal, strip)
    out_ref[PACKED - 16 : PACKED, :] = strip.astype(BF16)


def unpack(read, full_ref):
    row, col = rows_cols()
    for index, (a, b) in enumerate(BELOW):
        block = read(at(index))
        full_ref[at(a), at(b)] = block
        full_ref[at(b), at(a)] = block.T
    strip = read(slice(PACKED - 16, PACKED)).astype(F32)
    for pair in range(COLS // 2):
        both = read(at(len(BELOW) + pair)).astype(F32)
        turned = both.T
        first = jnp.where(row >= col, both, turned)
        second = jnp.where(row < col, both, turned)
        second = jnp.where(row == col, strip[pair : pair + 1, :], second)
        full_ref[at(2 * pair), at(2 * pair)] = first.astype(BF16)
        full_ref[at(2 * pair + 1), at(2 * pair + 1)] = second.astype(BF16)


def load(pairs, sems):
    copies = [pltpu.make_async_copy(source, target, sems.at[i]) for i, (source, target) in enumerate(pairs)]
    for copy in copies:
        copy.start()
    return copies


def pack_own(density, pattern, orbitals, out, counts, held, pattern_now, orbitals_now, sems):
    first = lax.axis_index(AXES) * COLS
    pairs = [(density.at[b, pl.ds(REACH, COLS - b)], held.at[b, pl.ds(0, COLS - b)]) for b in range(COLS)]
    copies = load([(orbitals, orbitals_now), (pattern, pattern_now)] + pairs, sems)
    row, col = rows_cols()
    for copy in copies[:2]:
        copy.wait()
    total = orbitals.shape[0]
    used = [orbitals_now[lax.rem(first + r - REACH + total, total)] for r in range(COLS + 2 * REACH)]
    seen = {}
    for c in range(COLS):
        for slot in range(BAND):
            seen[c, slot] = used[c + slot] * pattern_now[c, slot]
    for copy in copies[2:]:
        copy.wait()

    def block(a, b):
        visible = (row < seen[b, a - b + REACH]) & (col < used[b + REACH])
        return jnp.where(visible, held[b, a - b].astype(F32), 0.0)

    pack(out, block)
    for c in range(COLS):
        for slot in range(BAND):
            counts[count_row(c, slot), :] = jnp.full((1, T), seen[c, slot], jnp.int32)
        counts[COLS * BAND + c : COLS * BAND + c + 1, :] = jnp.full((1, T), used[c + REACH], jnp.int32)


def count_row(c, slot):
    return slice(c * BAND + slot, c * BAND + slot + 1)


def span(first, last):
    return slice(2 * first * T, 2 * (last + 1) * T)


RANGE = ((span(0, 1), span(1, 1)), (span(0, 0), span(0, 1)))
HALVES = (span(0, 0), span(1, 1))


def side_blocks(side):
    place = 0
    for c in range(COLS):
        for a in range(c, COLS) if side == 0 else range(c + 1):
            yield a, c, a - c + 2 * REACH * side, place
            place += 1


def keep(counts, c, slot):
    return counts[count_row(c, slot), :] > 0


def side_of(wide, side):
    return wide.at[side * 2 * SIDE : (side * 2 + 1) * SIDE]


def side_by_own(side, thin, own, out):
    if side == 0:
        out[HALVES[0], HALVES[0]] = dot(thin[HALVES[0], HALVES[0]], own[HALVES[0], HALVES[0]])
        out[HALVES[1], :] = dot(thin[HALVES[1], :], own[...])
    else:
        out[HALVES[0], :] = dot(thin[HALVES[0], :], own[...])
        out[HALVES[1], HALVES[1]] = dot(thin[HALVES[1], HALVES[1]], own[HALVES[1], HALVES[1]])


def full_by_side(side, half_col, full, thin):
    rows = RANGE[side][half_col]
    return dot(full[rows, rows], thin[rows, HALVES[half_col]])


def add_turned(side, left, right, before, out, lower=False):
    low, high = HALVES
    if side == 0:
        out[low, low] = before[low, low] + dot_tn(left[:, low], right[:, low])
        if not lower:
            out[low, high] = before[low, high] + dot_tn(left[high, low], right[high, high])
        out[high, :] = before[high, :] + dot_tn(left[high, high], right[high, :])
    else:
        inner = low if lower else slice(0, SIDE)
        out[low, inner] = before[low, inner] + dot_tn(left[low, low], right[low, inner])
        out[high, low] = before[high, low] + dot_tn(left[low, high], right[low, low])
        out[high, high] = before[high, high] + dot_tn(left[:, high], right[:, high])


def own_square(density, counts, packed_own, wide, square, squared, packed, both):
    row, col = rows_cols()
    zero = jnp.zeros((T, T), BF16)
    both[:PACKED, :] = packed_own[...]
    for c in range(COLS):
        in_cols = col < counts[COLS * BAND + c : COLS * BAND + c + 1, :]
        for r in range(COLS + 2 * REACH):
            if c <= r < c + BAND:
                visible = (row < counts[count_row(c, r - c), :]) & in_cols
                wide[at(r), at(c)] = jnp.where(visible, density[c, r - c].astype(F32), 0.0).astype(BF16)
            else:
                wide[at(r), at(c)] = zero
    own = wide.at[SIDE : 2 * SIDE]
    low, high = HALVES
    square[low, low] = dot(own[low, :], own[:, low])
    square[high, :] = dot(own[high, :], own[...])
    for side in range(2):
        add_turned(side, side_of(wide, side), side_of(wide, side), square, square, lower=True)
    for b in range(COLS):
        for a in range(b, COLS):
            block = jnp.where(keep(counts, b, a - b + REACH), square[at(a), at(b)], 0.0).astype(BF16)
            squared[at(a), at(b)] = block
    pack(packed, lambda a, b: squared[at(a), at(b)])
    both[PACKED:, :] = packed[...]


def own_products(wide, squared, local, cube, full):
    own = wide.at[SIDE : 2 * SIDE]
    full[...] = squared[...]
    for b in range(COLS):
        for a in range(b):
            full[at(a), at(b)] = squared[at(b), at(a)].T
    cube[...] = dot(full[...], own[...])
    for side in range(2):
        side_by_own(side, side_of(wide, side), own, local.at[side])


def by_side(turn, one):
    odd = lax.rem(lax.axis_index(AXES), 2)

    @pl.when(odd == turn)
    def _():
        one(1)

    @pl.when(odd != turn)
    def _():
        one(0)


def second_reader(swapped, to_last, offset):
    is_last = lax.axis_index(AXES) == lax.axis_size(AXES) - 1

    def read(rows):
        return jnp.where(is_last, to_last[rows.start + offset : rows.stop + offset, :], swapped[rows, :])

    return read


def cross_step(side, full, wide, counts, local, crossed, acc, before, cube):
    thin, own = side_of(wide, side), wide.at[SIDE : 2 * SIDE]
    for j in range(2):
        rows = RANGE[side][j]
        acc[rows, HALVES[j]] = local[side, rows, HALVES[j]] + full_by_side(side, j, full, thin)
    for a in range(COLS):
        for c in range(COLS):
            if (a >= c) if side == 0 else (a <= c):
                block = jnp.where(keep(counts, c, a - c + 2 * REACH * side), acc[at(a), at(c)], 0.0).astype(BF16)
            else:
                block = jnp.zeros((T, T), BF16)
            crossed[at(a), at(c)] = block
    low, high = HALVES
    for rows, inner, cols in (
        ((low, low, low), (high, slice(0, SIDE), slice(0, SIDE)))
        if side == 0
        else ((low, slice(0, SIDE), slice(0, SIDE)), (high, high, high))
    ):
        acc[rows, cols] = 3.0 * acc[rows, cols] - 2.0 * dot(crossed[rows, inner], own[inner, cols])
    add_turned(side, crossed, thin, before, cube)


def cross_first(packed, wide, counts, local, before, acc, cube, full, crossed):
    unpack(lambda rows: packed[rows, :], full)
    by_side(0, lambda side: cross_step(side, full, wide, counts, local, crossed, acc, before, cube))


def cross_second(packed, to_last, wide, counts, local, before, square, acc, out, cube, full, crossed, held, sems):
    unpack(second_reader(packed, to_last, 0), full)
    by_side(1, lambda side: cross_step(side, full, wide, counts, local, crossed, acc, before, cube))
    copies = []
    for c in range(COLS):
        for a in range(COLS):
            own = square[at(a), at(c)] if a // 2 >= c // 2 else square[at(c), at(a)].T
            mixed = 3.0 * own - 2.0 * cube[at(a), at(c)]
            held[c, a] = jnp.where(keep(counts, c, a - c + REACH), mixed, 0.0).astype(BF16)
        copies.append(pltpu.make_async_copy(held.at[c], out.at[c, pl.ds(REACH - c, COLS)], sems.at[c]))
        copies[-1].start()
    for copy in copies:
        copy.wait()


def finish(
    packed_first, packed_second, to_last, wide, counts, acc_first, acc_second, begun, out, full, held, sems
):
    del begun
    unpack(lambda rows: packed_first[rows, :], full.at[0])
    unpack(second_reader(packed_second, to_last, PACKED), full.at[1])

    def one(turn, acc, side):
        thin = side_of(wide, side)
        cross = [full_by_side(side, j, full.at[turn], thin) for j in range(2)]
        copies = []
        start = 0
        blocks = list(side_blocks(side))
        for c in range(COLS):
            here = [block for block in blocks if block[1] == c]
            for a, _, slot, place in here:
                top = a * T - RANGE[side][c // 2].start
                mixed = acc[at(a), at(c)] - 2.0 * cross[c // 2][top : top + T, at(c % 2)]
                held[turn, place] = jnp.where(keep(counts, c, slot), mixed, 0.0).astype(BF16)
            copies.append(
                pltpu.make_async_copy(
                    held.at[turn, pl.ds(here[0][3], len(here))],
                    out.at[c, pl.ds(here[0][2], len(here))],
                    sems.at[turn, c],
                )
            )
            copies[-1].start()
        return copies

    def both(side):
        for copy in one(0, acc_first, side) + one(1, acc_second, 1 - side):
            copy.wait()

    by_side(0, both)


def call(kernel, outs, ins, out_specs, scratch, flops, moved, **more):
    return pl.pallas_call(
        kernel,
        out_shape=outs,
        in_specs=ins,
        out_specs=out_specs,
        scratch_shapes=scratch,
        compiler_params=pltpu.CompilerParams(vmem_limit_bytes=LIMIT),
        cost_estimate=pl.CostEstimate(flops=flops, bytes_accessed=moved, transcendentals=0),
        **more,
    )


def shape(*dims, dtype=BF16):
    return jax.ShapeDtypeStruct(dims, dtype)


def per_device(density, pattern, orbitals):
    count = lax.axis_size(AXES)
    last = count - 1
    pairs = [(i, i ^ 1) for i in range(count)]
    others = [(i, (i + 1) % count if i % 2 else i - 1) for i in range(1, count)]

    def send(array, to):
        return lax.ppermute(array, AXES, to)

    far = [pltpu.with_memory_space_constraint(array, pltpu.HBM) for array in (density, pattern, orbitals)]
    whole = pltpu.VMEM((SIDE, SIDE), BF16)
    whole_f32 = shape(SIDE, SIDE, dtype=F32)
    packed, counts = call(
        pack_own,
        (shape(PACKED, T), shape(COLS * BAND + COLS, T, dtype=jnp.int32)),
        [ANY] * 3,
        (VMEM,) * 2,
        [
            pltpu.VMEM((COLS, COLS, T, T), BF16),
            pltpu.SMEM(pattern.shape, jnp.int32),
            pltpu.SMEM(orbitals.shape, jnp.int32),
            pltpu.SemaphoreType.DMA((COLS + 2,)),
        ],
        0,
        2**20,
    )(*far)
    own_first = send(packed, pairs)
    own_second = send(packed, others)
    wide, square, squared, packed_square, both = call(
        own_square,
        (shape(3 * SIDE, SIDE), whole_f32, shape(SIDE, SIDE), shape(PACKED, T), shape(2 * PACKED, T)),
        [VMEM] * 3,
        (VMEM,) * 5,
        [],
        2**30,
        2**22,
    )(density, counts, packed)
    square_first = send(packed_square, pairs)
    square_second = send(packed_square, others)
    to_last = send(both, [(0, last)])
    local, cube = call(
        own_products,
        (shape(2, SIDE, SIDE, dtype=F32), whole_f32),
        [VMEM] * 2,
        (VMEM,) * 2,
        [whole],
        17179869184,
        2**20,
    )(wide, squared)
    acc_first, cube = call(
        cross_first,
        (whole_f32, whole_f32),
        [VMEM] * 5,
        (VMEM, VMEM),
        [whole, whole],
        17179869184,
        2**20,
    )(own_first, wide, counts, local, cube)
    acc_second, begun = call(
        cross_second,
        (whole_f32, shape(*density.shape)),
        [VMEM] * 7,
        (VMEM, ANY),
        [
            pltpu.VMEM((SIDE, SIDE), F32),
            whole,
            whole,
            pltpu.VMEM((COLS, COLS, T, T), BF16),
            pltpu.SemaphoreType.DMA((COLS,)),
        ],
        2**30,
        2**21,
    )(own_second, to_last, wide, counts, local, cube, square)
    return call(
        finish,
        shape(*density.shape),
        [VMEM] * 7 + [ANY],
        ANY,
        [
            pltpu.VMEM((2, SIDE, SIDE), BF16),
            pltpu.VMEM((2, 10, T, T), BF16),
            pltpu.SemaphoreType.DMA((2, COLS)),
        ],
        2**28,
        2**21,
        input_output_aliases={7: 0},
    )(square_first, square_second, to_last, wide, counts, acc_first, acc_second, begun)


def solution(mesh):
    placed = (P(AXES, None, None, None), P(AXES, None), P())
    return jax.shard_map(
        per_device, mesh=mesh, in_specs=placed, out_specs=P(AXES, None, None, None), check_vma=False
    )
```

```python
import jax
import jax.numpy as jnp
from jax import lax
from jax.experimental import pallas as pl
from jax.experimental.pallas import tpu as pltpu
from jax.sharding import PartitionSpec as P

AXES = ("blk", "rep")
T = 128
COLS = 4
REACH = 4
BAND = 9
SIDE = COLS * T
BELOW = [(a, b) for b in range(COLS) for a in range(b + 1, COLS)]
PACKED = (len(BELOW) + COLS // 2) * T + 16
F32 = jnp.float32
BF16 = jnp.bfloat16
LIMIT = 40 * 1024 * 1024

VMEM = pl.BlockSpec(memory_space=pltpu.VMEM)
SMEM = pl.BlockSpec(memory_space=pltpu.SMEM)
ANY = pl.BlockSpec(memory_space=pl.ANY)


def rows_cols():
    return (
        lax.broadcasted_iota(jnp.int32, (T, T), 0),
        lax.broadcasted_iota(jnp.int32, (T, T), 1),
    )


def at(index):
    return slice(index * T, (index + 1) * T)


def dot(a, b):
    return lax.dot_general(a, b, (((1,), (0,)), ((), ())), preferred_element_type=F32)


def dot_tn(a, b):
    return lax.dot_general(a, b, (((0,), (0,)), ((), ())), preferred_element_type=F32)


def pack(out_ref, block):
    row, col = rows_cols()
    for index, (a, b) in enumerate(BELOW):
        out_ref[at(index), :] = block(a, b).astype(BF16)
    strip_row = lax.broadcasted_iota(jnp.int32, (16, T), 0)
    strip = jnp.zeros((16, T), F32)
    for pair in range(COLS // 2):
        first = block(2 * pair, 2 * pair).astype(F32)
        second = block(2 * pair + 1, 2 * pair + 1).astype(F32)
        out_ref[at(len(BELOW) + pair), :] = jnp.where(row >= col, first, second).astype(BF16)
        diagonal = jnp.sum(jnp.where(row == col, second, 0.0), axis=0, keepdims=True)
        strip = jnp.where(strip_row == pair, diagonal, strip)
    out_ref[PACKED - 16 : PACKED, :] = strip.astype(BF16)


def unpack(read, full_ref):
    row, col = rows_cols()
    for index, (a, b) in enumerate(BELOW):
        block = read(at(index))
        full_ref[at(a), at(b)] = block
        full_ref[at(b), at(a)] = block.T
    strip = read(slice(PACKED - 16, PACKED)).astype(F32)
    for pair in range(COLS // 2):
        both = read(at(len(BELOW) + pair)).astype(F32)
        turned = both.T
        first = jnp.where(row >= col, both, turned)
        second = jnp.where(row < col, both, turned)
        second = jnp.where(row == col, strip[pair : pair + 1, :], second)
        full_ref[at(2 * pair), at(2 * pair)] = first.astype(BF16)
        full_ref[at(2 * pair + 1), at(2 * pair + 1)] = second.astype(BF16)


def load(pairs, sems):
    copies = [pltpu.make_async_copy(source, target, sems.at[i]) for i, (source, target) in enumerate(pairs)]
    for copy in copies:
        copy.start()
    return copies


def count_row(c, slot):
    return slice(c * BAND + slot, c * BAND + slot + 1)


def span(first, last):
    return slice(2 * first * T, 2 * (last + 1) * T)


RANGE = ((span(0, 1), span(1, 1)), (span(0, 0), span(0, 1)))
HALVES = (span(0, 0), span(1, 1))


def side_blocks(side):
    place = 0
    for c in range(COLS):
        for a in range(c, COLS) if side == 0 else range(c + 1):
            yield a, c, a - c + 2 * REACH * side, place
            place += 1


def keep(counts, c, slot):
    return counts[count_row(c, slot), :] > 0


def side_of(wide, side):
    return wide.at[side * 2 * SIDE : (side * 2 + 1) * SIDE]


def side_by_own(side, thin, own, out):
    if side == 0:
        out[HALVES[0], HALVES[0]] = dot(thin[HALVES[0], HALVES[0]], own[HALVES[0], HALVES[0]])
        out[HALVES[1], :] = dot(thin[HALVES[1], :], own[...])
    else:
        out[HALVES[0], :] = dot(thin[HALVES[0], :], own[...])
        out[HALVES[1], HALVES[1]] = dot(thin[HALVES[1], HALVES[1]], own[HALVES[1], HALVES[1]])


def full_by_side(side, half_col, full, thin):
    rows = RANGE[side][half_col]
    return dot(full[rows, rows], thin[rows, HALVES[half_col]])


def add_turned(side, left, right, before, out, lower=False):
    low, high = HALVES
    if side == 0:
        out[low, low] = before[low, low] + dot_tn(left[:, low], right[:, low])
        if not lower:
            out[low, high] = before[low, high] + dot_tn(left[high, low], right[high, high])
        out[high, :] = before[high, :] + dot_tn(left[high, high], right[high, :])
    else:
        inner = low if lower else slice(0, SIDE)
        out[low, inner] = before[low, inner] + dot_tn(left[low, low], right[low, inner])
        out[high, low] = before[high, low] + dot_tn(left[low, high], right[low, low])
        out[high, high] = before[high, high] + dot_tn(left[:, high], right[:, high])


def own_square(
    density, pattern, orbitals, wide, counts, square, squared, both, held, pattern_now, orbitals_now, sems
):
    pairs = [(density.at[c], held.at[c]) for c in range(COLS)]
    copies = load([(orbitals, orbitals_now), (pattern, pattern_now)] + pairs, sems)
    row, col = rows_cols()
    zero = jnp.zeros((T, T), BF16)
    for c in range(COLS):
        for r in range(COLS + 2 * REACH):
            if not c <= r < c + BAND:
                wide[at(r), at(c)] = zero
    for copy in copies[:2]:
        copy.wait()
    first = lax.axis_index(AXES) * COLS
    total = orbitals.shape[0]
    used = [orbitals_now[lax.rem(first + r - REACH + total, total)] for r in range(COLS + 2 * REACH)]
    for c in range(COLS):
        seen = [used[c + slot] * pattern_now[c, slot] for slot in range(BAND)]
        copies[2 + c].wait()
        for slot in range(BAND):
            visible = (row < seen[slot]) & (col < used[c + REACH])
            wide[at(c + slot), at(c)] = jnp.where(visible, held[c, slot].astype(F32), 0.0).astype(BF16)
            counts[count_row(c, slot), :] = jnp.full((1, T), seen[slot], jnp.int32)
    own = wide.at[SIDE : 2 * SIDE]
    low, high = HALVES
    square[low, low] = dot(own[low, :], own[:, low])
    square[high, :] = dot(own[high, :], own[...])
    for side in range(2):
        add_turned(side, side_of(wide, side), side_of(wide, side), square, square, lower=True)
    pack(both.at[:PACKED], lambda a, b: own[at(a), at(b)])
    for b in range(COLS):
        for a in range(b, COLS):
            block = jnp.where(keep(counts, b, a - b + REACH), square[at(a), at(b)], 0.0).astype(BF16)
            squared[at(a), at(b)] = block
    pack(both.at[PACKED:], lambda a, b: squared[at(a), at(b)])


def own_products(wide, squared, local, cube, full):
    own = wide.at[SIDE : 2 * SIDE]
    full[...] = squared[...]
    for b in range(COLS):
        for a in range(b):
            full[at(a), at(b)] = squared[at(b), at(a)].T
    cube[...] = dot(full[...], own[...])
    for side in range(2):
        side_by_own(side, side_of(wide, side), own, local.at[side])


def by_side(turn, one):
    odd = lax.rem(lax.axis_index(AXES), 2)

    @pl.when(odd == turn)
    def _():
        one(1)

    @pl.when(odd != turn)
    def _():
        one(0)


def cross_step(side, full, wide, counts, local, crossed, acc, before, cube):
    thin = side_of(wide, side)
    for j in range(2):
        rows = RANGE[side][j]
        acc[rows, HALVES[j]] = local[side, rows, HALVES[j]] + full_by_side(side, j, full, thin)
    for a in range(COLS):
        for c in range(COLS):
            if (a >= c) if side == 0 else (a <= c):
                block = jnp.where(keep(counts, c, a - c + 2 * REACH * side), acc[at(a), at(c)], 0.0).astype(BF16)
            else:
                block = jnp.zeros((T, T), BF16)
            crossed[at(a), at(c)] = block
    add_turned(side, crossed, thin, before, cube)


def send_side(side, counts, held, out, sems, mixed):
    copies = []
    blocks = list(side_blocks(side))
    for c in range(COLS):
        here = [block for block in blocks if block[1] == c]
        for a, _, slot, place in here:
            held[place] = jnp.where(keep(counts, c, slot), mixed(a, c), 0.0).astype(BF16)
        copies.append(
            pltpu.make_async_copy(
                held.at[pl.ds(here[0][3], len(here))], out.at[c, pl.ds(here[0][2], len(here))], sems.at[c]
            )
        )
        copies[-1].start()
    return copies


def finish_side(turn, both, wide, counts, local, before, crossed, full, full_square, acc, cube, term, held, out, sems, copies_own):
    own = wide.at[SIDE : 2 * SIDE]
    unpack(lambda rows: both[rows, :], full)
    unpack(lambda rows: both[rows.start + PACKED : rows.stop + PACKED, :], full_square)

    def one(side):
        thin = side_of(wide, side)
        cross_step(side, full, wide, counts, local, crossed, acc, before, cube)
        copies = copies_own()
        side_by_own(side, crossed, own, term)
        for j in range(2):
            term[RANGE[side][j], HALVES[j]] += full_by_side(side, j, full_square, thin)
        copies += send_side(
            side, counts, held, out, sems, lambda a, c: 3.0 * acc[at(a), at(c)] - 2.0 * term[at(a), at(c)]
        )
        for copy in copies:
            copy.wait()

    by_side(turn, one)


def finish_first(both, wide, counts, local, before, out, cube, full, full_square, crossed, acc, term, held, sems):
    finish_side(0, both, wide, counts, local, before, crossed, full, full_square, acc, cube, term, held, out, sems, list)


def finish_second(
    both, wide, counts, local, before, square, begun, out, full, full_square, crossed, acc, term, held, sems, cube, held_own, sems_own
):
    del begun

    def copies_own():
        copies = []
        for c in range(COLS):
            for a in range(COLS):
                there = square[at(a), at(c)] if a // 2 >= c // 2 else square[at(c), at(a)].T
                mixed = 3.0 * there - 2.0 * cube[at(a), at(c)]
                held_own[c, a] = jnp.where(keep(counts, c, a - c + REACH), mixed, 0.0).astype(BF16)
            copies.append(pltpu.make_async_copy(held_own.at[c], out.at[c, pl.ds(REACH - c, COLS)], sems_own.at[c]))
            copies[-1].start()
        return copies

    finish_side(1, both, wide, counts, local, before, crossed, full, full_square, acc, cube, term, held, out, sems, copies_own)


def call(kernel, outs, ins, out_specs, scratch, flops, moved, **more):
    return pl.pallas_call(
        kernel,
        out_shape=outs,
        in_specs=ins,
        out_specs=out_specs,
        scratch_shapes=scratch,
        compiler_params=pltpu.CompilerParams(vmem_limit_bytes=LIMIT),
        cost_estimate=pl.CostEstimate(flops=flops, bytes_accessed=moved, transcendentals=0),
        **more,
    )


def shape(*dims, dtype=BF16):
    return jax.ShapeDtypeStruct(dims, dtype)


def per_device(density, pattern, orbitals):
    count = lax.axis_size(AXES)
    pairs = [(i, i ^ 1) for i in range(count)]
    others = [(i, (i + 1 if i % 2 else i - 1) % count) for i in range(count)]

    def send(array, to):
        return lax.ppermute(array, AXES, to)

    far = [pltpu.with_memory_space_constraint(array, pltpu.HBM) for array in (density, pattern, orbitals)]
    whole = pltpu.VMEM((SIDE, SIDE), BF16)
    whole_f32 = shape(SIDE, SIDE, dtype=F32)
    wide, counts, square, squared, both = call(
        own_square,
        (
            shape(3 * SIDE, SIDE),
            shape(COLS * BAND, T, dtype=jnp.int32),
            whole_f32,
            shape(SIDE, SIDE),
            shape(2 * PACKED, T),
        ),
        [ANY] * 3,
        (VMEM,) * 5,
        [
            pltpu.VMEM(density.shape, BF16),
            pltpu.SMEM(pattern.shape, jnp.int32),
            pltpu.SMEM(orbitals.shape, jnp.int32),
            pltpu.SemaphoreType.DMA((COLS + 2,)),
        ],
        2**30,
        2**22,
    )(*far)
    both_first = send(both, pairs)
    both_second = send(both, others)
    local, cube = call(
        own_products,
        (shape(2, SIDE, SIDE, dtype=F32), whole_f32),
        [VMEM] * 2,
        (VMEM,) * 2,
        [whole],
        2**29,
        2**20,
    )(wide, squared)
    total = pltpu.VMEM((SIDE, SIDE), F32)
    sems = pltpu.SemaphoreType.DMA((COLS,))
    room = [whole, whole, whole, total, total, pltpu.VMEM((10, T, T), BF16), sems]
    begun, cube = call(
        finish_first,
        (shape(*density.shape), whole_f32),
        [VMEM] * 5,
        (ANY, VMEM),
        room,
        2**31,
        2**21,
    )(both_first, wide, counts, local, cube)
    return call(
        finish_second,
        shape(*density.shape),
        [VMEM] * 6 + [ANY],
        ANY,
        [*room, total, pltpu.VMEM((COLS, COLS, T, T), BF16), sems],
        2**30,
        2**21,
        input_output_aliases={6: 0},
    )(both_second, wide, counts, local, cube, square, begun)


def solution(mesh):
    placed = (P(AXES, None, None, None), P(AXES, None), P())
    return jax.shard_map(
        per_device, mesh=mesh, in_specs=placed, out_specs=P(AXES, None, None, None), check_vma=False
    )
```

```python
import jax
import jax.numpy as jnp
from jax import lax
from jax.experimental import pallas as pl
from jax.experimental.pallas import tpu as pltpu
from jax.sharding import PartitionSpec as P

AXES = ("blk", "rep")
T = 128
COLS = 4
REACH = 4
BAND = 9
SIDE = COLS * T
BELOW = [(a, b) for b in range(COLS) for a in range(b + 1, COLS)]
PACKED = (len(BELOW) + COLS // 2) * T + 16
F32 = jnp.float32
BF16 = jnp.bfloat16
LIMIT = 40 * 1024 * 1024

VMEM = pl.BlockSpec(memory_space=pltpu.VMEM)
SMEM = pl.BlockSpec(memory_space=pltpu.SMEM)
ANY = pl.BlockSpec(memory_space=pl.ANY)


def rows_cols():
    return (
        lax.broadcasted_iota(jnp.int32, (T, T), 0),
        lax.broadcasted_iota(jnp.int32, (T, T), 1),
    )


def at(index):
    return slice(index * T, (index + 1) * T)


def dot(a, b):
    return lax.dot_general(a, b, (((1,), (0,)), ((), ())), preferred_element_type=F32)


def dot_tn(a, b):
    return lax.dot_general(a, b, (((0,), (0,)), ((), ())), preferred_element_type=F32)


def pack(out_ref, block):
    row, col = rows_cols()
    for index, (a, b) in enumerate(BELOW):
        out_ref[at(index), :] = block(a, b).astype(BF16)
    strip_row = lax.broadcasted_iota(jnp.int32, (16, T), 0)
    strip = jnp.zeros((16, T), F32)
    for pair in range(COLS // 2):
        first = block(2 * pair, 2 * pair).astype(F32)
        second = block(2 * pair + 1, 2 * pair + 1).astype(F32)
        out_ref[at(len(BELOW) + pair), :] = jnp.where(row >= col, first, second).astype(BF16)
        diagonal = jnp.sum(jnp.where(row == col, second, 0.0), axis=0, keepdims=True)
        strip = jnp.where(strip_row == pair, diagonal, strip)
    out_ref[PACKED - 16 : PACKED, :] = strip.astype(BF16)


def unpack(read, full_ref):
    row, col = rows_cols()
    for index, (a, b) in enumerate(BELOW):
        block = read(at(index))
        full_ref[at(a), at(b)] = block
        full_ref[at(b), at(a)] = block.T
    strip = read(slice(PACKED - 16, PACKED)).astype(F32)
    for pair in range(COLS // 2):
        both = read(at(len(BELOW) + pair)).astype(F32)
        turned = both.T
        first = jnp.where(row >= col, both, turned)
        second = jnp.where(row < col, both, turned)
        second = jnp.where(row == col, strip[pair : pair + 1, :], second)
        full_ref[at(2 * pair), at(2 * pair)] = first.astype(BF16)
        full_ref[at(2 * pair + 1), at(2 * pair + 1)] = second.astype(BF16)


def load(pairs, sems):
    copies = [pltpu.make_async_copy(source, target, sems.at[i]) for i, (source, target) in enumerate(pairs)]
    for copy in copies:
        copy.start()
    return copies


def count_row(c, slot):
    return slice(c * BAND + slot, c * BAND + slot + 1)


def span(first, last):
    return slice(2 * first * T, 2 * (last + 1) * T)


RANGE = ((span(0, 1), span(1, 1)), (span(0, 0), span(0, 1)))
HALVES = (span(0, 0), span(1, 1))


def side_blocks(side):
    place = 0
    for c in range(COLS):
        for a in range(c, COLS) if side == 0 else range(c + 1):
            yield a, c, a - c + 2 * REACH * side, place
            place += 1


def keep(counts, c, slot):
    return counts[count_row(c, slot), :] > 0


def side_of(wide, side):
    return wide.at[side * 2 * SIDE : (side * 2 + 1) * SIDE]


def side_by_own(side, thin, own, out):
    if side == 0:
        out[HALVES[0], HALVES[0]] = dot(thin[HALVES[0], HALVES[0]], own[HALVES[0], HALVES[0]])
        out[HALVES[1], :] = dot(thin[HALVES[1], :], own[...])
    else:
        out[HALVES[0], :] = dot(thin[HALVES[0], :], own[...])
        out[HALVES[1], HALVES[1]] = dot(thin[HALVES[1], HALVES[1]], own[HALVES[1], HALVES[1]])


def full_by_side(side, half_col, full, thin):
    rows = RANGE[side][half_col]
    return dot(full[rows, rows], thin[rows, HALVES[half_col]])


def add_turned(side, left, right, before, out, lower=False):
    low, high = HALVES
    if side == 0:
        out[low, low] = before[low, low] + dot_tn(left[:, low], right[:, low])
        if not lower:
            out[low, high] = before[low, high] + dot_tn(left[high, low], right[high, high])
        out[high, :] = before[high, :] + dot_tn(left[high, high], right[high, :])
    else:
        inner = low if lower else slice(0, SIDE)
        out[low, inner] = before[low, inner] + dot_tn(left[low, low], right[low, inner])
        out[high, low] = before[high, low] + dot_tn(left[low, high], right[low, low])
        out[high, high] = before[high, high] + dot_tn(left[:, high], right[:, high])


def own_square(
    density, pattern, orbitals, wide, counts, square, squared, both, longer, held, pattern_now, orbitals_now, sems
):
    pairs = [(density.at[c], held.at[c]) for c in range(COLS)]
    copies = load([(orbitals, orbitals_now), (pattern, pattern_now)] + pairs, sems)
    row, col = rows_cols()
    zero = jnp.zeros((T, T), BF16)
    for c in range(COLS):
        for r in range(COLS + 2 * REACH):
            if not c <= r < c + BAND:
                wide[at(r), at(c)] = zero
    for copy in copies[:2]:
        copy.wait()
    first = lax.axis_index(AXES) * COLS
    total = orbitals.shape[0]
    used = [orbitals_now[lax.rem(first + r - REACH + total, total)] for r in range(COLS + 2 * REACH)]
    for c in range(COLS):
        seen = [used[c + slot] * pattern_now[c, slot] for slot in range(BAND)]
        copies[2 + c].wait()
        for slot in range(BAND):
            visible = (row < seen[slot]) & (col < used[c + REACH])
            wide[at(c + slot), at(c)] = jnp.where(visible, held[c, slot].astype(F32), 0.0).astype(BF16)
            counts[count_row(c, slot), :] = jnp.full((1, T), seen[slot], jnp.int32)
    own = wide.at[SIDE : 2 * SIDE]
    low, high = HALVES
    square[low, low] = dot(own[low, :], own[:, low])
    square[high, :] = dot(own[high, :], own[...])
    for side in range(2):
        add_turned(side, side_of(wide, side), side_of(wide, side), square, square, lower=True)
    pack(both.at[:PACKED], lambda a, b: own[at(a), at(b)])
    for b in range(COLS):
        for a in range(b, COLS):
            block = jnp.where(keep(counts, b, a - b + REACH), square[at(a), at(b)], 0.0).astype(BF16)
            squared[at(a), at(b)] = block
    pack(both.at[PACKED:], lambda a, b: squared[at(a), at(b)])
    longer[: 2 * PACKED, :] = both[...]
    longer[2 * PACKED :, :] = jnp.zeros((16, T), BF16)


def own_products(wide, squared, local, cube, full):
    own = wide.at[SIDE : 2 * SIDE]
    full[...] = squared[...]
    for b in range(COLS):
        for a in range(b):
            full[at(a), at(b)] = squared[at(b), at(a)].T
    cube[...] = dot(full[...], own[...])
    for side in range(2):
        side_by_own(side, side_of(wide, side), own, local.at[side])


def by_side(turn, one):
    one(1 - turn)


def cross_step(side, full, wide, counts, local, crossed, acc, before, cube):
    thin = side_of(wide, side)
    for j in range(2):
        rows = RANGE[side][j]
        acc[rows, HALVES[j]] = local[side, rows, HALVES[j]] + full_by_side(side, j, full, thin)
    for a in range(COLS):
        for c in range(COLS):
            if (a >= c) if side == 0 else (a <= c):
                block = jnp.where(keep(counts, c, a - c + 2 * REACH * side), acc[at(a), at(c)], 0.0).astype(BF16)
            else:
                block = jnp.zeros((T, T), BF16)
            crossed[at(a), at(c)] = block
    add_turned(side, crossed, thin, before, cube)


def write_side(side, held, out, sems, start=True, columns=range(COLS)):
    copies = []
    blocks = list(side_blocks(side))
    for c in columns:
        here = [block for block in blocks if block[1] == c]
        copies.append(
            pltpu.make_async_copy(
                held.at[pl.ds(here[0][3], len(here))], out.at[c, pl.ds(here[0][2], len(here))], sems.at[c]
            )
        )
        if start:
            copies[-1].start()
    return copies


def finish_side(turn, both, wide, counts, local, before, full, terms, acc, cube, term, held, out, sems, copies_own, write):
    unpack(lambda rows: both[rows, :], full)

    def one(side):
        terms_square = terms.at[:, side * SIDE : (side + 1) * SIDE]
        crossed = terms.at[:, (1 - side) * SIDE : (2 - side) * SIDE]
        unpack(lambda rows: both[rows.start + PACKED : rows.stop + PACKED, :], terms_square)
        cross_step(side, full, wide, counts, local, crossed, acc, before, cube)
        copies = copies_own()
        for j in range(2):
            rows = RANGE[side][j]
            inner = slice(rows.start, 2 * SIDE) if side == 0 else slice(0, SIDE + rows.stop)
            below = slice(inner.start + side * SIDE, inner.stop + side * SIDE)
            term[rows, HALVES[j]] = dot(terms[rows, inner], wide[below, HALVES[j]])
            for a, c, slot, place in side_blocks(side):
                if c // 2 == j:
                    mixed = 3.0 * acc[at(a), at(c)] - 2.0 * term[at(a), at(c)]
                    held[place] = jnp.where(keep(counts, c, slot), mixed, 0.0).astype(BF16)
            copies += write_side(side, held, out, sems, columns=(2 * j, 2 * j + 1)) if write else []
        for copy in copies:
            copy.wait()

    by_side(turn, one)


def finish_first(both, wide, counts, local, before, held, cube, full, terms, acc, term):
    finish_side(0, both, wide, counts, local, before, full, terms, acc, cube, term, held, None, None, list, False)


def finish_second(
    both, wide, counts, local, before, square, first, out, full, terms, acc, term, held, sems, cube, held_own, sems_own, sems_first
):
    by_side(0, lambda side: write_side(side, first, out, sems_first) and None)

    def copies_own():
        copies = []
        for c in range(COLS):
            for a in range(COLS):
                there = square[at(a), at(c)] if a // 2 >= c // 2 else square[at(c), at(a)].T
                mixed = 3.0 * there - 2.0 * cube[at(a), at(c)]
                held_own[c, a] = jnp.where(keep(counts, c, a - c + REACH), mixed, 0.0).astype(BF16)
            copies.append(pltpu.make_async_copy(held_own.at[c], out.at[c, pl.ds(REACH - c, COLS)], sems_own.at[c]))
            copies[-1].start()
        return copies

    finish_side(1, both, wide, counts, local, before, full, terms, acc, cube, term, held, out, sems, copies_own, True)

    def first_done(side):
        for copy in write_side(side, first, out, sems_first, start=False):
            copy.wait()

    by_side(0, first_done)


def call(kernel, outs, ins, out_specs, scratch, flops, moved, **more):
    return pl.pallas_call(
        kernel,
        out_shape=outs,
        in_specs=ins,
        out_specs=out_specs,
        scratch_shapes=scratch,
        compiler_params=pltpu.CompilerParams(vmem_limit_bytes=LIMIT),
        cost_estimate=pl.CostEstimate(flops=flops, bytes_accessed=moved, transcendentals=0),
        **more,
    )


def shape(*dims, dtype=BF16):
    return jax.ShapeDtypeStruct(dims, dtype)


def per_device(density, pattern, orbitals):
    count = lax.axis_size(AXES)
    rightward = [(i, (i + 1) % count) for i in range(count)]
    leftward = [(i, (i - 1) % count) for i in range(count)]

    def send(array, to):
        return lax.ppermute(array, AXES, to)

    far = [pltpu.with_memory_space_constraint(array, pltpu.HBM) for array in (density, pattern, orbitals)]
    whole = pltpu.VMEM((SIDE, SIDE), BF16)
    whole_f32 = shape(SIDE, SIDE, dtype=F32)
    wide, counts, square, squared, both, longer = call(
        own_square,
        (
            shape(3 * SIDE, SIDE),
            shape(COLS * BAND, T, dtype=jnp.int32),
            whole_f32,
            shape(SIDE, SIDE),
            shape(2 * PACKED, T),
            shape(2 * PACKED + 16, T),
        ),
        [ANY] * 3,
        (VMEM,) * 6,
        [
            pltpu.VMEM(density.shape, BF16),
            pltpu.SMEM(pattern.shape, jnp.int32),
            pltpu.SMEM(orbitals.shape, jnp.int32),
            pltpu.SemaphoreType.DMA((COLS + 2,)),
        ],
        2**30,
        2**22,
    )(*far)
    both_left = send(longer, rightward)
    both_right = send(both, leftward)
    local, cube = call(
        own_products,
        (shape(2, SIDE, SIDE, dtype=F32), whole_f32),
        [VMEM] * 2,
        (VMEM,) * 2,
        [whole],
        2**29,
        2**20,
    )(wide, squared)
    total = pltpu.VMEM((SIDE, SIDE), F32)
    sems = pltpu.SemaphoreType.DMA((COLS,))
    room = [whole, pltpu.VMEM((SIDE, 2 * SIDE), BF16), total, total]
    first, cube = call(
        finish_first,
        (shape(10, T, T), whole_f32),
        [VMEM] * 5,
        (VMEM, VMEM),
        room,
        33554432,
        1024,
    )(both_right, wide, counts, local, cube)
    return call(
        finish_second,
        shape(*density.shape),
        [VMEM] * 7,
        ANY,
        [
            *room,
            pltpu.VMEM((10, T, T), BF16),
            sems,
            total,
            pltpu.VMEM((COLS, COLS, T, T), BF16),
            sems,
            sems,
        ],
        2**30,
        2**21,
    )(both_left, wide, counts, local, cube, square, first)


def solution(mesh):
    placed = (P(AXES, None, None, None), P(AXES, None), P())
    return jax.shard_map(
        per_device, mesh=mesh, in_specs=placed, out_specs=P(AXES, None, None, None), check_vma=False
    )
```

```python
import jax
import jax.numpy as jnp
from jax import lax
from jax.experimental import pallas as pl
from jax.experimental.pallas import tpu as pltpu
from jax.sharding import PartitionSpec as P

AXES = ("blk", "rep")
T = 128
COLS = 4
REACH = 4
BAND = 9
SIDE = COLS * T
BELOW = [(a, b) for b in range(COLS) for a in range(b + 1, COLS)]
PACKED = (len(BELOW) + COLS // 2) * T + 16
F32 = jnp.float32
BF16 = jnp.bfloat16
LIMIT = 40 * 1024 * 1024

VMEM = pl.BlockSpec(memory_space=pltpu.VMEM)
SMEM = pl.BlockSpec(memory_space=pltpu.SMEM)
ANY = pl.BlockSpec(memory_space=pl.ANY)


def rows_cols():
    return (
        lax.broadcasted_iota(jnp.int32, (T, T), 0),
        lax.broadcasted_iota(jnp.int32, (T, T), 1),
    )


def at(index):
    return slice(index * T, (index + 1) * T)


def dot(a, b):
    return lax.dot_general(a, b, (((1,), (0,)), ((), ())), preferred_element_type=F32)


def dot_tn(a, b):
    return lax.dot_general(a, b, (((0,), (0,)), ((), ())), preferred_element_type=F32)


def pack(out_ref, block):
    row, col = rows_cols()
    for index, (a, b) in enumerate(BELOW):
        out_ref[at(index), :] = block(a, b).astype(BF16)
    strip_row = lax.broadcasted_iota(jnp.int32, (16, T), 0)
    strip = jnp.zeros((16, T), F32)
    for pair in range(COLS // 2):
        first = block(2 * pair, 2 * pair).astype(F32)
        second = block(2 * pair + 1, 2 * pair + 1).astype(F32)
        out_ref[at(len(BELOW) + pair), :] = jnp.where(row >= col, first, second).astype(BF16)
        diagonal = jnp.sum(jnp.where(row == col, second, 0.0), axis=0, keepdims=True)
        strip = jnp.where(strip_row == pair, diagonal, strip)
    out_ref[PACKED - 16 : PACKED, :] = strip.astype(BF16)


def unpack(read, full_ref):
    row, col = rows_cols()
    for index, (a, b) in enumerate(BELOW):
        block = read(at(index))
        full_ref[at(a), at(b)] = block
        full_ref[at(b), at(a)] = block.T
    strip = read(slice(PACKED - 16, PACKED)).astype(F32)
    for pair in range(COLS // 2):
        both = read(at(len(BELOW) + pair)).astype(F32)
        turned = both.T
        first = jnp.where(row >= col, both, turned)
        second = jnp.where(row < col, both, turned)
        second = jnp.where(row == col, strip[pair : pair + 1, :], second)
        full_ref[at(2 * pair), at(2 * pair)] = first.astype(BF16)
        full_ref[at(2 * pair + 1), at(2 * pair + 1)] = second.astype(BF16)


def load(pairs, sems):
    copies = [pltpu.make_async_copy(source, target, sems.at[i]) for i, (source, target) in enumerate(pairs)]
    for copy in copies:
        copy.start()
    return copies


def count_row(c, slot):
    return slice(c * BAND + slot, c * BAND + slot + 1)


def span(first, last):
    return slice(2 * first * T, 2 * (last + 1) * T)


RANGE = ((span(0, 1), span(1, 1)), (span(0, 0), span(0, 1)))
HALVES = (span(0, 0), span(1, 1))


def side_blocks(side):
    place = 0
    for c in range(COLS):
        for a in range(c, COLS) if side == 0 else range(c + 1):
            yield a, c, a - c + 2 * REACH * side, place
            place += 1


def keep(counts, c, slot):
    return counts[count_row(c, slot), :] > 0


def side_of(wide, side):
    return wide.at[side * 2 * SIDE : (side * 2 + 1) * SIDE]


def side_by_own(side, thin, own, out):
    if side == 0:
        out[HALVES[0], HALVES[0]] = dot(thin[HALVES[0], HALVES[0]], own[HALVES[0], HALVES[0]])
        out[HALVES[1], :] = dot(thin[HALVES[1], :], own[...])
    else:
        out[HALVES[0], :] = dot(thin[HALVES[0], :], own[...])
        out[HALVES[1], HALVES[1]] = dot(thin[HALVES[1], HALVES[1]], own[HALVES[1], HALVES[1]])


def full_by_side(side, half_col, full, thin):
    rows = RANGE[side][half_col]
    return dot(full[rows, rows], thin[rows, HALVES[half_col]])


def add_turned(side, left, right, before, out, lower=False):
    low, high = HALVES
    if side == 0:
        out[low, low] = before[low, low] + dot_tn(left[:, low], right[:, low])
        if not lower:
            out[low, high] = before[low, high] + dot_tn(left[high, low], right[high, high])
        out[high, :] = before[high, :] + dot_tn(left[high, high], right[high, :])
    else:
        inner = low if lower else slice(0, SIDE)
        out[low, inner] = before[low, inner] + dot_tn(left[low, low], right[low, inner])
        out[high, low] = before[high, low] + dot_tn(left[low, high], right[low, low])
        out[high, high] = before[high, high] + dot_tn(left[:, high], right[:, high])


def own_square(
    density, pattern, orbitals, wide, counts, square, squared, both, longer, held, pattern_now, orbitals_now, sems
):
    pairs = [(density.at[c], held.at[c]) for c in range(COLS)]
    copies = load([(orbitals, orbitals_now), (pattern, pattern_now)] + pairs, sems)
    row, col = rows_cols()
    zero = jnp.zeros((T, T), BF16)
    for c in range(COLS):
        for r in range(COLS + 2 * REACH):
            if not c <= r < c + BAND:
                wide[at(r), at(c)] = zero
    for copy in copies[:2]:
        copy.wait()
    first = lax.axis_index(AXES) * COLS
    total = orbitals.shape[0]
    used = [orbitals_now[lax.rem(first + r - REACH + total, total)] for r in range(COLS + 2 * REACH)]
    left, own, right = (wide.at[k * SIDE : (k + 1) * SIDE] for k in range(3))
    low, high = HALVES
    for c in range(COLS):
        seen = [used[c + slot] * pattern_now[c, slot] for slot in range(BAND)]
        copies[2 + c].wait()
        for slot in range(BAND):
            visible = (row < seen[slot]) & (col < used[c + REACH])
            wide[at(c + slot), at(c)] = jnp.where(visible, held[c, slot].astype(F32), 0.0).astype(BF16)
            counts[count_row(c, slot), :] = jnp.full((1, T), seen[slot], jnp.int32)
    square[low, low] = (
        dot(own[low, :], own[:, low])
        + dot_tn(left[:, low], left[:, low])
        + dot_tn(right[low, low], right[low, low])
    )
    square[high, low] = (
        dot(own[high, :], own[:, low])
        + dot_tn(left[high, high], left[high, low])
        + dot_tn(right[low, high], right[low, low])
    )
    square[high, high] = (
        dot(own[high, :], own[:, high])
        + dot_tn(left[high, high], left[high, high])
        + dot_tn(right[:, high], right[:, high])
    )
    pack(both.at[:PACKED], lambda a, b: own[at(a), at(b)])
    for b in range(COLS):
        for a in range(b, COLS):
            block = jnp.where(keep(counts, b, a - b + REACH), square[at(a), at(b)], 0.0).astype(BF16)
            squared[at(a), at(b)] = block
    pack(both.at[PACKED:], lambda a, b: squared[at(a), at(b)])
    longer[: 2 * PACKED, :] = both[...]
    longer[2 * PACKED :, :] = jnp.zeros((16, T), BF16)


def own_products(wide, square, squared, local, base, full):
    own = wide.at[SIDE : 2 * SIDE]
    full[...] = squared[...]
    for b in range(COLS):
        for a in range(b):
            full[at(a), at(b)] = squared[at(b), at(a)].T
    base[...] = -2.0 * dot(full[...], own[...])
    for b in range(COLS):
        for a in range(COLS):
            there = square[at(a), at(b)] if a >= b else square[at(b), at(a)].T
            base[at(a), at(b)] += 3.0 * there
    for side in range(2):
        side_by_own(side, side_of(wide, side), own, local.at[side])


def turned_terms(side, left, right):
    low, high = HALVES
    if side == 0:
        yield 0, 0, dot_tn(left[:, low], right[:, low])
        yield 0, 2, dot_tn(left[high, low], right[high, high])
        yield 2, 0, dot_tn(left[high, high], right[high, :])
    else:
        yield 0, 0, dot_tn(left[low, low], right[low, :])
        yield 2, 0, dot_tn(left[low, high], right[low, low])
        yield 2, 2, dot_tn(left[:, high], right[:, high])


def write_side(side, held, out, sems):
    copies = []
    blocks = list(side_blocks(side))
    for c in range(COLS):
        here = [block for block in blocks if block[1] == c]
        copies.append(
            pltpu.make_async_copy(
                held.at[pl.ds(here[0][3], len(here))], out.at[c, pl.ds(here[0][2], len(here))], sems.at[c]
            )
        )
        copies[-1].start()
    return copies


def side_terms(side, both, wide, counts, local, full, square, crossed, acc, term, held):
    thin, own = side_of(wide, side), wide.at[SIDE : 2 * SIDE]
    unpack(lambda rows: both[rows, :], full)
    for j in range(2):
        rows = RANGE[side][j]
        acc[rows, HALVES[j]] = local[side, rows, HALVES[j]] + full_by_side(side, j, full, thin)
    unpack(lambda rows: both[rows.start + PACKED : rows.stop + PACKED, :], square)
    for j in range(2):
        term[RANGE[side][j], HALVES[j]] = full_by_side(side, j, square, thin)
    for a in range(COLS):
        for c in range(COLS):
            if (a >= c) if side == 0 else (a <= c):
                block = jnp.where(keep(counts, c, a - c + 2 * REACH * side), acc[at(a), at(c)], 0.0).astype(BF16)
            else:
                block = jnp.zeros((T, T), BF16)
            crossed[at(a), at(c)] = block
    low, high = HALVES
    every = slice(0, SIDE)
    for rows, inner, cols in (
        ((low, low, low), (high, every, every)) if side == 0 else ((low, every, every), (high, high, high))
    ):
        piece = dot(crossed[rows, inner], own[inner, cols])
        for a, c, slot, place in side_blocks(side):
            if rows.start <= a * T < rows.stop:
                here = piece[a * T - rows.start : (a + 1) * T - rows.start, c * T - cols.start : (c + 1) * T - cols.start]
                mixed = 3.0 * acc[at(a), at(c)] - 2.0 * (term[at(a), at(c)] + here)
                held[place] = jnp.where(keep(counts, c, slot), mixed, 0.0).astype(BF16)


def finish_first(both, wide, counts, local, before, held, base, full, square, crossed, acc, term):
    side_terms(1, both, wide, counts, local, full, square, crossed, acc, term, held)
    for first_row, first_col, piece in turned_terms(1, crossed, side_of(wide, 1)):
        rows = slice(first_row * T, first_row * T + piece.shape[0])
        cols = slice(first_col * T, first_col * T + piece.shape[1])
        base[rows, cols] = before[rows, cols] - 2.0 * piece


def finish_second(both, wide, counts, local, base, first, out, full, square, crossed, acc, term, held, sems, held_own, sems_own, sems_first):
    copies = write_side(1, first, out, sems_first)
    side_terms(0, both, wide, counts, local, full, square, crossed, acc, term, held)
    copies += write_side(0, held, out, sems)
    for first_row, first_col, piece in turned_terms(0, crossed, side_of(wide, 0)):
        for i in range(piece.shape[0] // T):
            for j in range(piece.shape[1] // T):
                a, c = first_row + i, first_col + j
                mixed = base[at(a), at(c)] - 2.0 * piece[at(i), at(j)]
                held_own[c, a] = jnp.where(keep(counts, c, a - c + REACH), mixed, 0.0).astype(BF16)
    for c in range(COLS):
        copies.append(pltpu.make_async_copy(held_own.at[c], out.at[c, pl.ds(REACH - c, COLS)], sems_own.at[c]))
        copies[-1].start()
    for copy in copies:
        copy.wait()


def call(kernel, outs, ins, out_specs, scratch, flops, moved, **more):
    return pl.pallas_call(
        kernel,
        out_shape=outs,
        in_specs=ins,
        out_specs=out_specs,
        scratch_shapes=scratch,
        compiler_params=pltpu.CompilerParams(vmem_limit_bytes=LIMIT),
        cost_estimate=pl.CostEstimate(flops=flops, bytes_accessed=moved, transcendentals=0),
        **more,
    )


def shape(*dims, dtype=BF16):
    return jax.ShapeDtypeStruct(dims, dtype)


def per_device(density, pattern, orbitals):
    count = lax.axis_size(AXES)
    rightward = [(i, (i + 1) % count) for i in range(count)]
    leftward = [(i, (i - 1) % count) for i in range(count)]

    def send(array, to):
        return lax.ppermute(array, AXES, to)

    far = [pltpu.with_memory_space_constraint(array, pltpu.HBM) for array in (density, pattern, orbitals)]
    whole = pltpu.VMEM((SIDE, SIDE), BF16)
    whole_f32 = shape(SIDE, SIDE, dtype=F32)
    wide, counts, square, squared, both, longer = call(
        own_square,
        (
            shape(3 * SIDE, SIDE),
            shape(COLS * BAND, T, dtype=jnp.int32),
            whole_f32,
            shape(SIDE, SIDE),
            shape(2 * PACKED, T),
            shape(2 * PACKED + 16, T),
        ),
        [ANY] * 3,
        (VMEM,) * 6,
        [
            pltpu.VMEM(density.shape, BF16),
            pltpu.SMEM(pattern.shape, jnp.int32),
            pltpu.SMEM(orbitals.shape, jnp.int32),
            pltpu.SemaphoreType.DMA((COLS + 2,)),
        ],
        2**30,
        2**22,
    )(*far)
    both_left = send(longer, rightward)
    both_right = send(both, leftward)
    local, base = call(
        own_products,
        (shape(2, SIDE, SIDE, dtype=F32), whole_f32),
        [VMEM] * 3,
        (VMEM,) * 2,
        [whole],
        2**29,
        2**20,
    )(wide, square, squared)
    sems = pltpu.SemaphoreType.DMA((COLS,))
    total = pltpu.VMEM((SIDE, SIDE), F32)
    room = [whole, whole, whole, total, total]
    ten = pltpu.VMEM((10, T, T), BF16)
    first, base = call(
        finish_first,
        (shape(10, T, T), whole_f32),
        [VMEM] * 5,
        (VMEM, VMEM),
        room,
        2**25,
        2**10,
    )(both_right, wide, counts, local, base)
    return call(
        finish_second,
        shape(*density.shape),
        [VMEM] * 6,
        ANY,
        [*room, ten, sems, pltpu.VMEM((COLS, COLS, T, T), BF16), sems, sems],
        2**30,
        2**21,
    )(both_left, wide, counts, local, base, first)


def solution(mesh):
    placed = (P(AXES, None, None, None), P(AXES, None), P())
    return jax.shard_map(
        per_device, mesh=mesh, in_specs=placed, out_specs=P(AXES, None, None, None), check_vma=False
    )
```

```python
import jax
import jax.numpy as jnp
from jax import lax
from jax.experimental import pallas as pl
from jax.experimental.pallas import tpu as pltpu
from jax.sharding import PartitionSpec as P

AXES = ("blk", "rep")
T = 128
COLS = 4
REACH = 4
BAND = 9
SIDE = COLS * T
BELOW = [(a, b) for b in range(COLS) for a in range(b + 1, COLS)]
PACKED = (len(BELOW) + COLS // 2) * T
SENT = 2 * PACKED + 16
F32 = jnp.float32
BF16 = jnp.bfloat16
LIMIT = 40 * 1024 * 1024

VMEM = pl.BlockSpec(memory_space=pltpu.VMEM)
SMEM = pl.BlockSpec(memory_space=pltpu.SMEM)
ANY = pl.BlockSpec(memory_space=pl.ANY)


def rows_cols():
    return (
        lax.broadcasted_iota(jnp.int32, (T, T), 0),
        lax.broadcasted_iota(jnp.int32, (T, T), 1),
    )


def at(index):
    return slice(index * T, (index + 1) * T)


def dot(a, b):
    return lax.dot_general(a, b, (((1,), (0,)), ((), ())), preferred_element_type=F32)


def dot_tn(a, b):
    return lax.dot_general(a, b, (((0,), (0,)), ((), ())), preferred_element_type=F32)


def pack(outs, offset, block):
    row, col = rows_cols()

    def put(first_row, value):
        for out in outs:
            out[offset + first_row : offset + first_row + value.shape[0], :] = value.astype(BF16)

    for index, (a, b) in enumerate(BELOW):
        put(index * T, block(a, b))
    diagonals = []
    for pair in range(COLS // 2):
        first = block(2 * pair, 2 * pair).astype(F32)
        second = block(2 * pair + 1, 2 * pair + 1).astype(F32)
        put((len(BELOW) + pair) * T, jnp.where(row >= col, first, second))
        diagonals.append(jnp.sum(jnp.where(row == col, second, 0.0), axis=0, keepdims=True))
    return diagonals


def unpack(both, which, full_ref):
    def read(rows):
        return both[rows.start + which * PACKED : rows.stop + which * PACKED, :]

    row, col = rows_cols()
    for index, (a, b) in enumerate(BELOW):
        block = read(at(index))
        full_ref[at(a), at(b)] = block
        full_ref[at(b), at(a)] = block.T
    strip = both[2 * PACKED : SENT, :].astype(F32)
    for pair in range(COLS // 2):
        two = read(at(len(BELOW) + pair)).astype(F32)
        turned = two.T
        first = jnp.where(row >= col, two, turned)
        second = jnp.where(row < col, two, turned)
        second = jnp.where(row == col, strip[2 * which + pair : 2 * which + pair + 1, :], second)
        full_ref[at(2 * pair), at(2 * pair)] = first.astype(BF16)
        full_ref[at(2 * pair + 1), at(2 * pair + 1)] = second.astype(BF16)


def load(pairs, sems):
    copies = [pltpu.make_async_copy(source, target, sems.at[i]) for i, (source, target) in enumerate(pairs)]
    for copy in copies:
        copy.start()
    return copies


def count_row(c, slot):
    return slice(c * BAND + slot, c * BAND + slot + 1)


def span(first, last):
    return slice(2 * first * T, 2 * (last + 1) * T)


RANGE = ((span(0, 1), span(1, 1)), (span(0, 0), span(0, 1)))
HALVES = (span(0, 0), span(1, 1))


def side_blocks(side):
    place = 0
    for c in range(COLS):
        for a in range(c, COLS) if side == 0 else range(c + 1):
            yield a, c, a - c + 2 * REACH * side, place
            place += 1


def keep(counts, c, slot):
    return counts[count_row(c, slot), :] > 0


def side_of(wide, side):
    return wide.at[side * 2 * SIDE : (side * 2 + 1) * SIDE]


def side_by_own(side, thin, own, out):
    if side == 0:
        out[HALVES[0], HALVES[0]] = dot(thin[HALVES[0], HALVES[0]], own[HALVES[0], HALVES[0]])
        out[HALVES[1], :] = dot(thin[HALVES[1], :], own[...])
    else:
        out[HALVES[0], :] = dot(thin[HALVES[0], :], own[...])
        out[HALVES[1], HALVES[1]] = dot(thin[HALVES[1], HALVES[1]], own[HALVES[1], HALVES[1]])


def full_by_side(side, half_col, full, thin):
    rows = RANGE[side][half_col]
    return dot(full[rows, rows], thin[rows, HALVES[half_col]])


def add_turned(side, left, right, before, out, lower=False):
    low, high = HALVES
    if side == 0:
        out[low, low] = before[low, low] + dot_tn(left[:, low], right[:, low])
        if not lower:
            out[low, high] = before[low, high] + dot_tn(left[high, low], right[high, high])
        out[high, :] = before[high, :] + dot_tn(left[high, high], right[high, :])
    else:
        inner = low if lower else slice(0, SIDE)
        out[low, inner] = before[low, inner] + dot_tn(left[low, low], right[low, inner])
        out[high, low] = before[high, low] + dot_tn(left[low, high], right[low, low])
        out[high, high] = before[high, high] + dot_tn(left[:, high], right[:, high])


def own_square(
    density, pattern, orbitals, wide, counts, square, squared, both, longer, held, pattern_now, orbitals_now, sems
):
    pairs = [(density.at[c], held.at[c]) for c in range(COLS)]
    copies = load([(orbitals, orbitals_now), (pattern, pattern_now)] + pairs, sems)
    row, col = rows_cols()
    zero = jnp.zeros((T, T), BF16)
    for c in range(COLS):
        for r in range(COLS + 2 * REACH):
            if not c <= r < c + BAND:
                wide[at(r), at(c)] = zero
    for copy in copies[:2]:
        copy.wait()
    first = lax.axis_index(AXES) * COLS
    total = orbitals.shape[0]
    used = [orbitals_now[lax.rem(first + r - REACH + total, total)] for r in range(COLS + 2 * REACH)]
    left, own, right = (wide.at[k * SIDE : (k + 1) * SIDE] for k in range(3))
    low, high = HALVES
    for c in range(COLS):
        seen = [used[c + slot] * pattern_now[c, slot] for slot in range(BAND)]
        copies[2 + c].wait()
        for slot in range(BAND):
            visible = (row < seen[slot]) & (col < used[c + REACH])
            wide[at(c + slot), at(c)] = jnp.where(visible, held[c, slot].astype(F32), 0.0).astype(BF16)
            counts[count_row(c, slot), :] = jnp.full((1, T), seen[slot], jnp.int32)
    diagonals = pack((both, longer), 0, lambda a, b: own[at(a), at(b)])
    square[low, low] = (
        dot(own[low, :], own[:, low])
        + dot_tn(left[:, low], left[:, low])
        + dot_tn(right[low, low], right[low, low])
    )
    square[high, low] = (
        dot(own[high, :], own[:, low])
        + dot_tn(left[high, high], left[high, low])
        + dot_tn(right[low, high], right[low, low])
    )
    square[high, high] = (
        dot(own[high, :], own[:, high])
        + dot_tn(left[high, high], left[high, high])
        + dot_tn(right[:, high], right[:, high])
    )
    for b in range(COLS):
        for a in range(b, COLS):
            block = jnp.where(keep(counts, b, a - b + REACH), square[at(a), at(b)], 0.0).astype(BF16)
            squared[at(a), at(b)] = block
    diagonals += pack((both, longer), PACKED, lambda a, b: squared[at(a), at(b)])
    strip_row = lax.broadcasted_iota(jnp.int32, (16, T), 0)
    strip = jnp.zeros((16, T), F32)
    for index, diagonal in enumerate(diagonals):
        strip = jnp.where(strip_row == index, diagonal, strip)
    both[2 * PACKED : SENT, :] = strip.astype(BF16)
    longer[2 * PACKED : SENT, :] = strip.astype(BF16)
    longer[SENT:, :] = jnp.zeros((16, T), BF16)


def own_products(wide, square, squared, local, base, full):
    own = wide.at[SIDE : 2 * SIDE]
    full[...] = squared[...]
    for b in range(COLS):
        for a in range(b):
            full[at(a), at(b)] = squared[at(b), at(a)].T
    base[...] = -2.0 * dot(full[...], own[...])
    for b in range(COLS):
        for a in range(COLS):
            there = square[at(a), at(b)] if a >= b else square[at(b), at(a)].T
            base[at(a), at(b)] += 3.0 * there
    for side in range(2):
        side_by_own(side, side_of(wide, side), own, local.at[side])


def turned_terms(side, left, right):
    low, high = HALVES
    if side == 0:
        yield 0, 0, dot_tn(left[:, low], right[:, low])
        yield 0, 2, dot_tn(left[high, low], right[high, high])
        yield 2, 0, dot_tn(left[high, high], right[high, :])
    else:
        yield 0, 0, dot_tn(left[low, low], right[low, :])
        yield 2, 0, dot_tn(left[low, high], right[low, low])
        yield 2, 2, dot_tn(left[:, high], right[:, high])


def write_side(side, held, out, sems):
    copies = []
    blocks = list(side_blocks(side))
    for c in range(COLS):
        here = [block for block in blocks if block[1] == c]
        copies.append(
            pltpu.make_async_copy(
                held.at[pl.ds(here[0][3], len(here))], out.at[c, pl.ds(here[0][2], len(here))], sems.at[c]
            )
        )
        copies[-1].start()
    return copies


def side_terms(side, both, wide, counts, local, full, square, crossed, acc, term, held):
    thin, own = side_of(wide, side), wide.at[SIDE : 2 * SIDE]
    unpack(both, 0, full)
    for j in range(2):
        rows = RANGE[side][j]
        acc[rows, HALVES[j]] = local[side, rows, HALVES[j]] + full_by_side(side, j, full, thin)
    unpack(both, 1, square)
    for j in range(2):
        term[RANGE[side][j], HALVES[j]] = full_by_side(side, j, square, thin)
    for a in range(COLS):
        for c in range(COLS):
            if (a >= c) if side == 0 else (a <= c):
                block = jnp.where(keep(counts, c, a - c + 2 * REACH * side), acc[at(a), at(c)], 0.0).astype(BF16)
            else:
                block = jnp.zeros((T, T), BF16)
            crossed[at(a), at(c)] = block
    low, high = HALVES
    every = slice(0, SIDE)
    for rows, inner, cols in (
        ((low, low, low), (high, every, every)) if side == 0 else ((low, every, every), (high, high, high))
    ):
        piece = dot(crossed[rows, inner], own[inner, cols])
        for a, c, slot, place in side_blocks(side):
            if rows.start <= a * T < rows.stop:
                here = piece[a * T - rows.start : (a + 1) * T - rows.start, c * T - cols.start : (c + 1) * T - cols.start]
                mixed = 3.0 * acc[at(a), at(c)] - 2.0 * (term[at(a), at(c)] + here)
                held[place] = jnp.where(keep(counts, c, slot), mixed, 0.0).astype(BF16)


def finish_first(both, wide, counts, local, before, held, base, full, square, crossed, acc, term):
    side_terms(1, both, wide, counts, local, full, square, crossed, acc, term, held)
    for first_row, first_col, piece in turned_terms(1, crossed, side_of(wide, 1)):
        rows = slice(first_row * T, first_row * T + piece.shape[0])
        cols = slice(first_col * T, first_col * T + piece.shape[1])
        base[rows, cols] = before[rows, cols] - 2.0 * piece


def finish_second(both, wide, counts, local, base, first, out, full, square, crossed, acc, term, held, sems, held_own, sems_own, sems_first):
    copies = write_side(1, first, out, sems_first)
    side_terms(0, both, wide, counts, local, full, square, crossed, acc, term, held)
    copies += write_side(0, held, out, sems)
    for first_row, first_col, piece in turned_terms(0, crossed, side_of(wide, 0)):
        for i in range(piece.shape[0] // T):
            for j in range(piece.shape[1] // T):
                a, c = first_row + i, first_col + j
                mixed = base[at(a), at(c)] - 2.0 * piece[at(i), at(j)]
                held_own[c, a] = jnp.where(keep(counts, c, a - c + REACH), mixed, 0.0).astype(BF16)
    for c in range(COLS):
        copies.append(pltpu.make_async_copy(held_own.at[c], out.at[c, pl.ds(REACH - c, COLS)], sems_own.at[c]))
        copies[-1].start()
    for copy in copies:
        copy.wait()


def call(kernel, outs, ins, out_specs, scratch, flops, moved, **more):
    return pl.pallas_call(
        kernel,
        out_shape=outs,
        in_specs=ins,
        out_specs=out_specs,
        scratch_shapes=scratch,
        compiler_params=pltpu.CompilerParams(vmem_limit_bytes=LIMIT),
        cost_estimate=pl.CostEstimate(flops=flops, bytes_accessed=moved, transcendentals=0),
        **more,
    )


def shape(*dims, dtype=BF16):
    return jax.ShapeDtypeStruct(dims, dtype)


def per_device(density, pattern, orbitals):
    count = lax.axis_size(AXES)
    rightward = [(i, (i + 1) % count) for i in range(count)]
    leftward = [(i, (i - 1) % count) for i in range(count)]

    def send(array, to):
        return lax.ppermute(array, AXES, to)

    far = [pltpu.with_memory_space_constraint(array, pltpu.HBM) for array in (density, pattern, orbitals)]
    whole = pltpu.VMEM((SIDE, SIDE), BF16)
    whole_f32 = shape(SIDE, SIDE, dtype=F32)
    wide, counts, square, squared, both, longer = call(
        own_square,
        (
            shape(3 * SIDE, SIDE),
            shape(COLS * BAND, T, dtype=jnp.int32),
            whole_f32,
            shape(SIDE, SIDE),
            shape(SENT, T),
            shape(SENT + 16, T),
        ),
        [ANY] * 3,
        (VMEM,) * 6,
        [
            pltpu.VMEM(density.shape, BF16),
            pltpu.SMEM(pattern.shape, jnp.int32),
            pltpu.SMEM(orbitals.shape, jnp.int32),
            pltpu.SemaphoreType.DMA((COLS + 2,)),
        ],
        2**30,
        2**22,
    )(*far)
    both_left = send(longer, rightward)
    both_right = send(both, leftward)
    local, base = call(
        own_products,
        (shape(2, SIDE, SIDE, dtype=F32), whole_f32),
        [VMEM] * 3,
        (VMEM,) * 2,
        [whole],
        2**29,
        2**20,
    )(wide, square, squared)
    sems = pltpu.SemaphoreType.DMA((COLS,))
    total = pltpu.VMEM((SIDE, SIDE), F32)
    room = [whole, whole, whole, total, total]
    ten = pltpu.VMEM((10, T, T), BF16)
    first, base = call(
        finish_first,
        (shape(10, T, T), whole_f32),
        [VMEM] * 5,
        (VMEM, VMEM),
        room,
        2**25,
        2**10,
    )(both_right, wide, counts, local, base)
    return call(
        finish_second,
        shape(*density.shape),
        [VMEM] * 6,
        ANY,
        [*room, ten, sems, pltpu.VMEM((COLS, COLS, T, T), BF16), sems, sems],
        2**30,
        2**21,
    )(both_left, wide, counts, local, base, first)


def solution(mesh):
    placed = (P(AXES, None, None, None), P(AXES, None), P())
    return jax.shard_map(
        per_device, mesh=mesh, in_specs=placed, out_specs=P(AXES, None, None, None), check_vma=False
    )
```

```python
import jax
import jax.numpy as jnp
from jax import lax
from jax.experimental import pallas as pl
from jax.experimental.pallas import tpu as pltpu
from jax.sharding import PartitionSpec as P

AXES = ("blk", "rep")
T = 128
COLS = 4
REACH = 4
BAND = 9
SIDE = COLS * T
BELOW = [(a, b) for b in range(COLS) for a in range(b + 1, COLS)]
PACKED = (len(BELOW) + COLS // 2) * T
SENT = 2 * PACKED + 16
F32 = jnp.float32
BF16 = jnp.bfloat16
LIMIT = 40 * 1024 * 1024

VMEM = pl.BlockSpec(memory_space=pltpu.VMEM)
SMEM = pl.BlockSpec(memory_space=pltpu.SMEM)
ANY = pl.BlockSpec(memory_space=pl.ANY)


def rows_cols():
    return (
        lax.broadcasted_iota(jnp.int32, (T, T), 0),
        lax.broadcasted_iota(jnp.int32, (T, T), 1),
    )


def at(index):
    return slice(index * T, (index + 1) * T)


def dot(a, b):
    return lax.dot_general(a, b, (((1,), (0,)), ((), ())), preferred_element_type=F32)


def dot_tn(a, b):
    return lax.dot_general(a, b, (((0,), (0,)), ((), ())), preferred_element_type=F32)


def pack(outs, offset, block):
    row, col = rows_cols()

    def put(first_row, value):
        for out in outs:
            out[offset + first_row : offset + first_row + value.shape[0], :] = value.astype(BF16)

    for index, (a, b) in enumerate(BELOW):
        put(index * T, block(a, b))
    diagonals = []
    for pair in range(COLS // 2):
        first = block(2 * pair, 2 * pair).astype(F32)
        second = block(2 * pair + 1, 2 * pair + 1).astype(F32)
        put((len(BELOW) + pair) * T, jnp.where(row >= col, first, second))
        diagonals.append(jnp.sum(jnp.where(row == col, second, 0.0), axis=0, keepdims=True))
    return diagonals


def unpack(both, which, full_ref):
    def read(rows):
        return both[rows.start + which * PACKED : rows.stop + which * PACKED, :]

    row, col = rows_cols()
    for index, (a, b) in enumerate(BELOW):
        block = read(at(index))
        full_ref[at(a), at(b)] = block
        full_ref[at(b), at(a)] = block.T
    strip = both[2 * PACKED : SENT, :].astype(F32)
    for pair in range(COLS // 2):
        two = read(at(len(BELOW) + pair)).astype(F32)
        turned = two.T
        first = jnp.where(row >= col, two, turned)
        second = jnp.where(row < col, two, turned)
        second = jnp.where(row == col, strip[2 * which + pair : 2 * which + pair + 1, :], second)
        full_ref[at(2 * pair), at(2 * pair)] = first.astype(BF16)
        full_ref[at(2 * pair + 1), at(2 * pair + 1)] = second.astype(BF16)


def load(pairs, sems):
    copies = [pltpu.make_async_copy(source, target, sems.at[i]) for i, (source, target) in enumerate(pairs)]
    for copy in copies:
        copy.start()
    return copies


def count_row(c, slot):
    return slice(c * BAND + slot, c * BAND + slot + 1)


def span(first, last):
    return slice(2 * first * T, 2 * (last + 1) * T)


RANGE = ((span(0, 1), span(1, 1)), (span(0, 0), span(0, 1)))
HALVES = (span(0, 0), span(1, 1))


def side_blocks(side):
    place = 0
    for c in range(COLS):
        for a in range(c, COLS) if side == 0 else range(c + 1):
            yield a, c, a - c + 2 * REACH * side, place
            place += 1


def keep(counts, c, slot):
    return counts[count_row(c, slot), :] > 0


def side_of(wide, side):
    return wide.at[side * 2 * SIDE : (side * 2 + 1) * SIDE]


def side_by_own(side, thin, own, out):
    if side == 0:
        out[HALVES[0], HALVES[0]] = dot(thin[HALVES[0], HALVES[0]], own[HALVES[0], HALVES[0]])
        out[HALVES[1], :] = dot(thin[HALVES[1], :], own[...])
    else:
        out[HALVES[0], :] = dot(thin[HALVES[0], :], own[...])
        out[HALVES[1], HALVES[1]] = dot(thin[HALVES[1], HALVES[1]], own[HALVES[1], HALVES[1]])


def full_by_side(side, half_col, full, thin):
    rows = RANGE[side][half_col]
    return dot(full[rows, rows], thin[rows, HALVES[half_col]])


def add_turned(side, left, right, before, out, lower=False):
    low, high = HALVES
    if side == 0:
        out[low, low] = before[low, low] + dot_tn(left[:, low], right[:, low])
        if not lower:
            out[low, high] = before[low, high] + dot_tn(left[high, low], right[high, high])
        out[high, :] = before[high, :] + dot_tn(left[high, high], right[high, :])
    else:
        inner = low if lower else slice(0, SIDE)
        out[low, inner] = before[low, inner] + dot_tn(left[low, low], right[low, inner])
        out[high, low] = before[high, low] + dot_tn(left[low, high], right[low, low])
        out[high, high] = before[high, high] + dot_tn(left[:, high], right[:, high])


def own_square(
    density, pattern, orbitals, wide, counts, square, squared, both, longer, held, pattern_now, orbitals_now, sems
):
    pairs = [(density.at[c], held.at[c]) for c in range(COLS)]
    copies = load([(orbitals, orbitals_now), (pattern, pattern_now)] + pairs, sems)
    row, col = rows_cols()
    zero = jnp.zeros((T, T), BF16)
    for c in range(COLS):
        for r in range(COLS + 2 * REACH):
            if not c <= r < c + BAND:
                wide[at(r), at(c)] = zero
    for copy in copies[:2]:
        copy.wait()
    first = lax.axis_index(AXES) * COLS
    total = orbitals.shape[0]
    used = [orbitals_now[lax.rem(first + r - REACH + total, total)] for r in range(COLS + 2 * REACH)]
    left, own, right = (wide.at[k * SIDE : (k + 1) * SIDE] for k in range(3))
    low, high = HALVES
    for c in range(COLS):
        seen = [used[c + slot] * pattern_now[c, slot] for slot in range(BAND)]
        copies[2 + c].wait()
        for slot in range(BAND):
            visible = (row < seen[slot]) & (col < used[c + REACH])
            wide[at(c + slot), at(c)] = jnp.where(visible, held[c, slot].astype(F32), 0.0).astype(BF16)
            counts[count_row(c, slot), :] = jnp.full((1, T), seen[slot], jnp.int32)
    diagonals = pack((both, longer), 0, lambda a, b: own[at(a), at(b)])
    square[low, low] = (
        dot(own[low, :], own[:, low])
        + dot_tn(left[:, low], left[:, low])
        + dot_tn(right[low, low], right[low, low])
    )
    square[high, low] = (
        dot(own[high, :], own[:, low])
        + dot_tn(left[high, high], left[high, low])
        + dot_tn(right[low, high], right[low, low])
    )
    square[high, high] = (
        dot(own[high, :], own[:, high])
        + dot_tn(left[high, high], left[high, high])
        + dot_tn(right[:, high], right[:, high])
    )
    for b in range(COLS):
        for a in range(b, COLS):
            block = jnp.where(keep(counts, b, a - b + REACH), square[at(a), at(b)], 0.0).astype(BF16)
            squared[at(a), at(b)] = block
    diagonals += pack((both, longer), PACKED, lambda a, b: squared[at(a), at(b)])
    strip_row = lax.broadcasted_iota(jnp.int32, (16, T), 0)
    strip = jnp.zeros((16, T), F32)
    for index, diagonal in enumerate(diagonals):
        strip = jnp.where(strip_row == index, diagonal, strip)
    both[2 * PACKED : SENT, :] = strip.astype(BF16)
    longer[2 * PACKED : SENT, :] = strip.astype(BF16)
    longer[SENT:, :] = jnp.zeros((16, T), BF16)


def own_products(wide, square, squared, local, base, full):
    own = wide.at[SIDE : 2 * SIDE]
    full[...] = squared[...]
    for b in range(COLS):
        for a in range(b):
            full[at(a), at(b)] = squared[at(b), at(a)].T
    base[...] = -2.0 * dot(full[...], own[...])
    for b in range(COLS):
        for a in range(COLS):
            there = square[at(a), at(b)] if a >= b else square[at(b), at(a)].T
            base[at(a), at(b)] += 3.0 * there
    for side in range(2):
        side_by_own(side, side_of(wide, side), own, local.at[side])


def turned_terms(side, left, right):
    low, high = HALVES
    if side == 0:
        yield 0, 0, dot_tn(left[:, low], right[:, low])
        yield 0, 2, dot_tn(left[high, low], right[high, high])
        yield 2, 0, dot_tn(left[high, high], right[high, :])
    else:
        yield 0, 0, dot_tn(left[low, low], right[low, :])
        yield 2, 0, dot_tn(left[low, high], right[low, low])
        yield 2, 2, dot_tn(left[:, high], right[:, high])


def write_side(side, held, out, sems):
    copies = []
    blocks = list(side_blocks(side))
    for c in range(COLS):
        here = [block for block in blocks if block[1] == c]
        copies.append(
            pltpu.make_async_copy(
                held.at[pl.ds(here[0][3], len(here))], out.at[c, pl.ds(here[0][2], len(here))], sems.at[c]
            )
        )
        copies[-1].start()
    return copies


def side_terms(side, both, wide, counts, local, full, square, crossed, acc, term, held):
    thin, own = side_of(wide, side), wide.at[SIDE : 2 * SIDE]
    unpack(both, 0, full)
    unpack(both, 1, square)
    for j in range(2):
        rows = RANGE[side][j]
        acc[rows, HALVES[j]] = local[side, rows, HALVES[j]] + full_by_side(side, j, full, thin)
    for j in range(2):
        term[RANGE[side][j], HALVES[j]] = full_by_side(side, j, square, thin)
    for c in range(COLS):
        for a in range(COLS):
            if (a >= c) if side == 0 else (a <= c):
                block = jnp.where(keep(counts, c, a - c + 2 * REACH * side), acc[at(a), at(c)], 0.0).astype(BF16)
                crossed[at(a), at(c)] = block
            elif a // 2 == c // 2:
                crossed[at(a), at(c)] = jnp.zeros((T, T), BF16)
    low, high = HALVES
    every = slice(0, SIDE)
    for rows, inner, cols in (
        ((low, low, low), (high, every, every)) if side == 0 else ((low, every, every), (high, high, high))
    ):
        piece = dot(crossed[rows, inner], own[inner, cols])
        for a, c, slot, place in side_blocks(side):
            if rows.start <= a * T < rows.stop:
                here = piece[a * T - rows.start : (a + 1) * T - rows.start, c * T - cols.start : (c + 1) * T - cols.start]
                mixed = 3.0 * acc[at(a), at(c)] - 2.0 * (term[at(a), at(c)] + here)
                held[place] = jnp.where(keep(counts, c, slot), mixed, 0.0).astype(BF16)


def finish_first(both, wide, counts, local, before, held, base, full, square, crossed, acc, term):
    side_terms(1, both, wide, counts, local, full, square, crossed, acc, term, held)
    for first_row, first_col, piece in turned_terms(1, crossed, side_of(wide, 1)):
        rows = slice(first_row * T, first_row * T + piece.shape[0])
        cols = slice(first_col * T, first_col * T + piece.shape[1])
        base[rows, cols] = before[rows, cols] - 2.0 * piece


def finish_second(both, wide, counts, local, base, first, out, full, square, crossed, acc, term, held, sems, held_own, sems_own, sems_first):
    copies = write_side(1, first, out, sems_first)
    side_terms(0, both, wide, counts, local, full, square, crossed, acc, term, held)
    copies += write_side(0, held, out, sems)
    for first_row, first_col, piece in turned_terms(0, crossed, side_of(wide, 0)):
        for i in range(piece.shape[0] // T):
            for j in range(piece.shape[1] // T):
                a, c = first_row + i, first_col + j
                mixed = base[at(a), at(c)] - 2.0 * piece[at(i), at(j)]
                held_own[c, a] = jnp.where(keep(counts, c, a - c + REACH), mixed, 0.0).astype(BF16)
    for c in range(COLS):
        copies.append(pltpu.make_async_copy(held_own.at[c], out.at[c, pl.ds(REACH - c, COLS)], sems_own.at[c]))
        copies[-1].start()
    for copy in copies:
        copy.wait()


def call(kernel, outs, ins, out_specs, scratch, flops, moved, **more):
    return pl.pallas_call(
        kernel,
        out_shape=outs,
        in_specs=ins,
        out_specs=out_specs,
        scratch_shapes=scratch,
        compiler_params=pltpu.CompilerParams(vmem_limit_bytes=LIMIT),
        cost_estimate=pl.CostEstimate(flops=flops, bytes_accessed=moved, transcendentals=0),
        **more,
    )


def shape(*dims, dtype=BF16):
    return jax.ShapeDtypeStruct(dims, dtype)


def per_device(density, pattern, orbitals):
    count = lax.axis_size(AXES)
    rightward = [(i, (i + 1) % count) for i in range(count)]
    leftward = [(i, (i - 1) % count) for i in range(count)]

    def send(array, to):
        return lax.ppermute(array, AXES, to)

    far = [pltpu.with_memory_space_constraint(array, pltpu.HBM) for array in (density, pattern, orbitals)]
    whole = pltpu.VMEM((SIDE, SIDE), BF16)
    whole_f32 = shape(SIDE, SIDE, dtype=F32)
    wide, counts, square, squared, both, longer = call(
        own_square,
        (
            shape(3 * SIDE, SIDE),
            shape(COLS * BAND, T, dtype=jnp.int32),
            whole_f32,
            shape(SIDE, SIDE),
            shape(SENT, T),
            shape(SENT + 16, T),
        ),
        [ANY] * 3,
        (VMEM,) * 6,
        [
            pltpu.VMEM(density.shape, BF16),
            pltpu.SMEM(pattern.shape, jnp.int32),
            pltpu.SMEM(orbitals.shape, jnp.int32),
            pltpu.SemaphoreType.DMA((COLS + 2,)),
        ],
        2**30,
        2**22,
    )(*far)
    both_left = send(longer, rightward)
    both_right = send(both, leftward)
    local, base = call(
        own_products,
        (shape(2, SIDE, SIDE, dtype=F32), whole_f32),
        [VMEM] * 3,
        (VMEM,) * 2,
        [whole],
        2**29,
        2**20,
    )(wide, square, squared)
    sems = pltpu.SemaphoreType.DMA((COLS,))
    total = pltpu.VMEM((SIDE, SIDE), F32)
    room = [whole, whole, whole, total, total]
    ten = pltpu.VMEM((10, T, T), BF16)
    first, base = call(
        finish_first,
        (shape(10, T, T), whole_f32),
        [VMEM] * 5,
        (VMEM, VMEM),
        room,
        2**25,
        2**10,
    )(both_right, wide, counts, local, base)
    return call(
        finish_second,
        shape(*density.shape),
        [VMEM] * 6,
        ANY,
        [*room, ten, sems, pltpu.VMEM((COLS, COLS, T, T), BF16), sems, sems],
        2**30,
        2**21,
    )(both_left, wide, counts, local, base, first)


def solution(mesh):
    placed = (P(AXES, None, None, None), P(AXES, None), P())
    return jax.shard_map(
        per_device, mesh=mesh, in_specs=placed, out_specs=P(AXES, None, None, None), check_vma=False
    )
```

```python
import jax
import jax.numpy as jnp
from jax import lax
from jax.experimental import pallas as pl
from jax.experimental.pallas import tpu as pltpu
from jax.sharding import PartitionSpec as P

AXES = ("blk", "rep")
T = 128
COLS = 4
REACH = 4
BAND = 9
SIDE = COLS * T
BELOW = [(a, b) for b in range(COLS) for a in range(b + 1, COLS)]
PACKED = (len(BELOW) + COLS // 2) * T
SENT = 2 * PACKED + 16
F32 = jnp.float32
BF16 = jnp.bfloat16
LIMIT = 40 * 1024 * 1024

VMEM = pl.BlockSpec(memory_space=pltpu.VMEM)
SMEM = pl.BlockSpec(memory_space=pltpu.SMEM)
ANY = pl.BlockSpec(memory_space=pl.ANY)


def rows_cols():
    return (
        lax.broadcasted_iota(jnp.int32, (T, T), 0),
        lax.broadcasted_iota(jnp.int32, (T, T), 1),
    )


def at(index):
    return slice(index * T, (index + 1) * T)


def dot(a, b):
    return lax.dot_general(a, b, (((1,), (0,)), ((), ())), preferred_element_type=F32)


def dot_tn(a, b):
    return lax.dot_general(a, b, (((0,), (0,)), ((), ())), preferred_element_type=F32)


def pack(outs, offset, block):
    row, col = rows_cols()

    def put(first_row, value):
        for out in outs:
            out[offset + first_row : offset + first_row + value.shape[0], :] = value.astype(BF16)

    for index, (a, b) in enumerate(BELOW):
        put(index * T, block(a, b))
    diagonals = []
    for pair in range(COLS // 2):
        first = block(2 * pair, 2 * pair).astype(F32)
        second = block(2 * pair + 1, 2 * pair + 1).astype(F32)
        put((len(BELOW) + pair) * T, jnp.where(row >= col, first, second))
        diagonals.append(jnp.sum(jnp.where(row == col, second, 0.0), axis=0, keepdims=True))
    return diagonals


def unpack(both, which, full_ref):
    def read(rows):
        return both[rows.start + which * PACKED : rows.stop + which * PACKED, :]

    row, col = rows_cols()
    for index, (a, b) in enumerate(BELOW):
        block = read(at(index))
        full_ref[at(a), at(b)] = block
        full_ref[at(b), at(a)] = block.astype(F32).T.astype(BF16)
    strip = both[2 * PACKED : SENT, :].astype(F32)
    for pair in range(COLS // 2):
        two = read(at(len(BELOW) + pair)).astype(F32)
        turned = two.T
        first = jnp.where(row >= col, two, turned)
        second = jnp.where(row < col, two, turned)
        second = jnp.where(row == col, strip[2 * which + pair : 2 * which + pair + 1, :], second)
        full_ref[at(2 * pair), at(2 * pair)] = first.astype(BF16)
        full_ref[at(2 * pair + 1), at(2 * pair + 1)] = second.astype(BF16)


def load(pairs, sems):
    copies = [pltpu.make_async_copy(source, target, sems.at[i]) for i, (source, target) in enumerate(pairs)]
    for copy in copies:
        copy.start()
    return copies


def count_row(c, slot):
    return slice(c * BAND + slot, c * BAND + slot + 1)


def span(first, last):
    return slice(2 * first * T, 2 * (last + 1) * T)


RANGE = ((span(0, 1), span(1, 1)), (span(0, 0), span(0, 1)))
HALVES = (span(0, 0), span(1, 1))


def side_blocks(side):
    place = 0
    for c in range(COLS):
        for a in range(c, COLS) if side == 0 else range(c + 1):
            yield a, c, a - c + 2 * REACH * side, place
            place += 1


def keep(counts, c, slot):
    return counts[count_row(c, slot), :] > 0


def side_of(wide, side):
    return wide.at[side * 2 * SIDE : (side * 2 + 1) * SIDE]


def side_by_own(side, thin, own, out):
    if side == 0:
        out[HALVES[0], HALVES[0]] = dot(thin[HALVES[0], HALVES[0]], own[HALVES[0], HALVES[0]])
        out[HALVES[1], :] = dot(thin[HALVES[1], :], own[...])
    else:
        out[HALVES[0], :] = dot(thin[HALVES[0], :], own[...])
        out[HALVES[1], HALVES[1]] = dot(thin[HALVES[1], HALVES[1]], own[HALVES[1], HALVES[1]])


def full_by_side(side, half_col, full, thin):
    rows = RANGE[side][half_col]
    return dot(full[rows, rows], thin[rows, HALVES[half_col]])


def add_turned(side, left, right, before, out, lower=False):
    low, high = HALVES
    if side == 0:
        out[low, low] = before[low, low] + dot_tn(left[:, low], right[:, low])
        if not lower:
            out[low, high] = before[low, high] + dot_tn(left[high, low], right[high, high])
        out[high, :] = before[high, :] + dot_tn(left[high, high], right[high, :])
    else:
        inner = low if lower else slice(0, SIDE)
        out[low, inner] = before[low, inner] + dot_tn(left[low, low], right[low, inner])
        out[high, low] = before[high, low] + dot_tn(left[low, high], right[low, low])
        out[high, high] = before[high, high] + dot_tn(left[:, high], right[:, high])


def own_square(
    density, pattern, orbitals, wide, counts, square, squared, both, longer, held, pattern_now, orbitals_now, sems
):
    pairs = [(density.at[c], held.at[c]) for c in range(COLS)]
    copies = load([(orbitals, orbitals_now), (pattern, pattern_now)] + pairs, sems)
    row, col = rows_cols()
    zero = jnp.zeros((T, T), BF16)
    for c in range(COLS):
        for r in range(COLS + 2 * REACH):
            if not c <= r < c + BAND:
                wide[at(r), at(c)] = zero
    for copy in copies[:2]:
        copy.wait()
    first = lax.axis_index(AXES) * COLS
    total = orbitals.shape[0]
    used = [orbitals_now[lax.rem(first + r - REACH + total, total)] for r in range(COLS + 2 * REACH)]
    left, own, right = (wide.at[k * SIDE : (k + 1) * SIDE] for k in range(3))
    low, high = HALVES
    for c in range(COLS):
        seen = [used[c + slot] * pattern_now[c, slot] for slot in range(BAND)]
        copies[2 + c].wait()
        for slot in range(BAND):
            visible = (row < seen[slot]) & (col < used[c + REACH])
            wide[at(c + slot), at(c)] = jnp.where(visible, held[c, slot].astype(F32), 0.0).astype(BF16)
            counts[count_row(c, slot), :] = jnp.full((1, T), seen[slot], jnp.int32)
    diagonals = pack((both, longer), 0, lambda a, b: own[at(a), at(b)])
    square[low, low] = (
        dot(own[low, :], own[:, low])
        + dot_tn(left[:, low], left[:, low])
        + dot_tn(right[low, low], right[low, low])
    )
    square[high, low] = (
        dot(own[high, :], own[:, low])
        + dot_tn(left[high, high], left[high, low])
        + dot_tn(right[low, high], right[low, low])
    )
    square[high, high] = (
        dot(own[high, :], own[:, high])
        + dot_tn(left[high, high], left[high, high])
        + dot_tn(right[:, high], right[:, high])
    )
    for b in range(COLS):
        for a in range(b, COLS):
            block = jnp.where(keep(counts, b, a - b + REACH), square[at(a), at(b)], 0.0).astype(BF16)
            squared[at(a), at(b)] = block
    diagonals += pack((both, longer), PACKED, lambda a, b: squared[at(a), at(b)])
    strip_row = lax.broadcasted_iota(jnp.int32, (16, T), 0)
    strip = jnp.zeros((16, T), F32)
    for index, diagonal in enumerate(diagonals):
        strip = jnp.where(strip_row == index, diagonal, strip)
    both[2 * PACKED : SENT, :] = strip.astype(BF16)
    longer[2 * PACKED : SENT, :] = strip.astype(BF16)
    longer[SENT:, :] = jnp.zeros((16, T), BF16)


def own_products(wide, square, squared, local, base, full):
    own = wide.at[SIDE : 2 * SIDE]
    full[...] = squared[...]
    for b in range(COLS):
        for a in range(b):
            full[at(a), at(b)] = squared[at(b), at(a)].T
    base[...] = -2.0 * dot(full[...], own[...])
    for b in range(COLS):
        for a in range(COLS):
            there = square[at(a), at(b)] if a >= b else square[at(b), at(a)].T
            base[at(a), at(b)] += 3.0 * there
    for side in range(2):
        side_by_own(side, side_of(wide, side), own, local.at[side])


def turned_terms(side, left, right):
    low, high = HALVES
    if side == 0:
        yield 0, 0, dot_tn(left[:, low], right[:, low])
        yield 0, 2, dot_tn(left[high, low], right[high, high])
        yield 2, 0, dot_tn(left[high, high], right[high, :])
    else:
        yield 0, 0, dot_tn(left[low, low], right[low, :])
        yield 2, 0, dot_tn(left[low, high], right[low, low])
        yield 2, 2, dot_tn(left[:, high], right[:, high])


def write_side(side, held, out, sems):
    copies = []
    blocks = list(side_blocks(side))
    for c in range(COLS):
        here = [block for block in blocks if block[1] == c]
        copies.append(
            pltpu.make_async_copy(
                held.at[pl.ds(here[0][3], len(here))], out.at[c, pl.ds(here[0][2], len(here))], sems.at[c]
            )
        )
        copies[-1].start()
    return copies


def side_terms(side, both, wide, counts, local, full, square, crossed, acc, term, held):
    thin, own = side_of(wide, side), wide.at[SIDE : 2 * SIDE]
    unpack(both, 0, full)
    unpack(both, 1, square)
    for j in range(2):
        rows = RANGE[side][j]
        acc[rows, HALVES[j]] = local[side, rows, HALVES[j]] + full_by_side(side, j, full, thin)
    for j in range(2):
        term[RANGE[side][j], HALVES[j]] = full_by_side(side, j, square, thin)
    for c in range(COLS):
        for a in range(COLS):
            if (a >= c) if side == 0 else (a <= c):
                block = jnp.where(keep(counts, c, a - c + 2 * REACH * side), acc[at(a), at(c)], 0.0).astype(BF16)
                crossed[at(a), at(c)] = block
            elif a // 2 == c // 2:
                crossed[at(a), at(c)] = jnp.zeros((T, T), BF16)
    low, high = HALVES
    every = slice(0, SIDE)
    for rows, inner, cols in (
        ((low, low, low), (high, every, every)) if side == 0 else ((low, every, every), (high, high, high))
    ):
        piece = dot(crossed[rows, inner], own[inner, cols])
        for a, c, slot, place in side_blocks(side):
            if rows.start <= a * T < rows.stop:
                here = piece[a * T - rows.start : (a + 1) * T - rows.start, c * T - cols.start : (c + 1) * T - cols.start]
                mixed = 3.0 * acc[at(a), at(c)] - 2.0 * (term[at(a), at(c)] + here)
                held[place] = jnp.where(keep(counts, c, slot), mixed, 0.0).astype(BF16)


def finish_first(both, wide, counts, local, before, held, base, full, square, crossed, acc, term):
    side_terms(1, both, wide, counts, local, full, square, crossed, acc, term, held)
    for first_row, first_col, piece in turned_terms(1, crossed, side_of(wide, 1)):
        rows = slice(first_row * T, first_row * T + piece.shape[0])
        cols = slice(first_col * T, first_col * T + piece.shape[1])
        base[rows, cols] = before[rows, cols] - 2.0 * piece


def finish_second(both, wide, counts, local, base, first, out, full, square, crossed, acc, term, held, sems, held_own, sems_own, sems_first):
    copies = write_side(1, first, out, sems_first)
    side_terms(0, both, wide, counts, local, full, square, crossed, acc, term, held)
    copies += write_side(0, held, out, sems)
    for first_row, first_col, piece in turned_terms(0, crossed, side_of(wide, 0)):
        for i in range(piece.shape[0] // T):
            for j in range(piece.shape[1] // T):
                a, c = first_row + i, first_col + j
                mixed = base[at(a), at(c)] - 2.0 * piece[at(i), at(j)]
                held_own[c, a] = jnp.where(keep(counts, c, a - c + REACH), mixed, 0.0).astype(BF16)
    for c in range(COLS):
        copies.append(pltpu.make_async_copy(held_own.at[c], out.at[c, pl.ds(REACH - c, COLS)], sems_own.at[c]))
        copies[-1].start()
    for copy in copies:
        copy.wait()


def call(kernel, outs, ins, out_specs, scratch, flops, moved, **more):
    return pl.pallas_call(
        kernel,
        out_shape=outs,
        in_specs=ins,
        out_specs=out_specs,
        scratch_shapes=scratch,
        compiler_params=pltpu.CompilerParams(vmem_limit_bytes=LIMIT),
        cost_estimate=pl.CostEstimate(flops=flops, bytes_accessed=moved, transcendentals=0),
        **more,
    )


def shape(*dims, dtype=BF16):
    return jax.ShapeDtypeStruct(dims, dtype)


def per_device(density, pattern, orbitals):
    count = lax.axis_size(AXES)
    rightward = [(i, (i + 1) % count) for i in range(count)]
    leftward = [(i, (i - 1) % count) for i in range(count)]

    def send(array, to):
        return lax.ppermute(array, AXES, to)

    far = [pltpu.with_memory_space_constraint(array, pltpu.HBM) for array in (density, pattern, orbitals)]
    whole = pltpu.VMEM((SIDE, SIDE), BF16)
    whole_f32 = shape(SIDE, SIDE, dtype=F32)
    wide, counts, square, squared, both, longer = call(
        own_square,
        (
            shape(3 * SIDE, SIDE),
            shape(COLS * BAND, T, dtype=jnp.int32),
            whole_f32,
            shape(SIDE, SIDE),
            shape(SENT, T),
            shape(SENT + 16, T),
        ),
        [ANY] * 3,
        (VMEM,) * 6,
        [
            pltpu.VMEM(density.shape, BF16),
            pltpu.SMEM(pattern.shape, jnp.int32),
            pltpu.SMEM(orbitals.shape, jnp.int32),
            pltpu.SemaphoreType.DMA((COLS + 2,)),
        ],
        2**30,
        2**22,
    )(*far)
    both_left = send(longer, rightward)
    both_right = send(both, leftward)
    local, base = call(
        own_products,
        (shape(2, SIDE, SIDE, dtype=F32), whole_f32),
        [VMEM] * 3,
        (VMEM,) * 2,
        [whole],
        2**29,
        2**20,
    )(wide, square, squared)
    sems = pltpu.SemaphoreType.DMA((COLS,))
    total = pltpu.VMEM((SIDE, SIDE), F32)
    room = [whole, whole, whole, total, total]
    ten = pltpu.VMEM((10, T, T), BF16)
    first, base = call(
        finish_first,
        (shape(10, T, T), whole_f32),
        [VMEM] * 5,
        (VMEM, VMEM),
        room,
        2**25,
        2**10,
    )(both_right, wide, counts, local, base)
    return call(
        finish_second,
        shape(*density.shape),
        [VMEM] * 6,
        ANY,
        [*room, ten, sems, pltpu.VMEM((COLS, COLS, T, T), BF16), sems, sems],
        2**30,
        2**21,
    )(both_left, wide, counts, local, base, first)


def solution(mesh):
    placed = (P(AXES, None, None, None), P(AXES, None), P())
    return jax.shard_map(
        per_device, mesh=mesh, in_specs=placed, out_specs=P(AXES, None, None, None), check_vma=False
    )
```
